512 devices in a mesh: dom: 64 (over z, x, core), feat: 8 (over y).
Axes of the slice: x: 4, y: 8, z: 8, core: 2. Of those that a mesh axis runs over, the one named last changes fastest.
Arguments:
- first_layer: bfloat16 [32768, 1024], P('dom', 'feat'), may hold values from -6 to 6
- w_first: bfloat16 [1024, 1024], P('feat', 'dom'), may hold values from -0.1875 to 0.1875
- w_second: bfloat16 [1024, 1024], P('feat', 'dom'), may hold values from -0.1875 to 0.1875
- tile_values: bfloat16 [256, 10, 128, 128], P('dom'), may hold values from -0.15625 to 0.15625
- tile_sources: int32 [64, 4, 10], P('dom'), may hold values from 0 to 35, as said below
- halo_sources: int32 [64, 32], P('dom'), may hold values from 0 to 63, as said below
- send_rows: int32 [64, 64, 128], P('dom'), may hold values from 0 to 512, as said below
- block_counts: int32 [64, 64], P('dom'), may hold values from 0 to 1, as said below
- stale_halo: bfloat16 [262144, 1024], P('dom', 'feat'), may hold values from 0 to 2
Outputs:
- layer_out: bfloat16 [32768, 1024], P('dom', 'feat')
- fresh_halo: bfloat16 [262144, 1024], P('dom', 'feat')
The draws below stay inside these ranges and needn't reach their ends.
Inputs may be any that keep to these rules, and one draw needn't show every extreme that they name: `tile_sources`: tile 0 of row block i has source i (a local block), tile 1 a local block, the others halo blocks: 4 + j stands for halo block j; every halo block is read by some tile of its partition. `halo_sources`: row p lists 32 distinct partitions other than p, in increasing order. block_counts[q, p] is 1 exactly where q is listed in row p of halo_sources, else 0. `send_rows`: within one block the live rows come first and are distinct rows of the sending partition; the value 512 marks a padding slot.
All inputs are finite; a program needn't handle non-finite values.
Results may differ from the reference program's by a relative error of at most 0.014.
Values may be sent and summed in bfloat16 or wider, within the bound.
No kernel may reach another device: no remote copies, remote signals or barrier semaphores. Data moves between devices by JAX's collectives and lax.ppermute only.
A program may use at most 64 MiB of HBM per device.

```python
import math
import jax
import jax.numpy as jnp
from jax import lax

D = 1024
BLOCK = 128
TILES = 10
ROWS = 512
NB = 4
HALO = 32
NODES = 32768
N_DOM = 64
N_FEAT = 8


def peer_lists(key):
    key = jax.random.fold_in(key, 5)
    scores = jax.random.randint(key, (N_DOM, N_DOM - 1), 0, 2 ** 18, dtype=jnp.int32)
    scores = scores * N_DOM + jnp.arange(N_DOM - 1, dtype=jnp.int32)[None, :]
    offsets = jnp.argsort(scores, axis=-1, stable=True)[:, :HALO].astype(jnp.int32)
    owners = jnp.arange(N_DOM, dtype=jnp.int32)[:, None]
    peers = (owners + 1 + offsets) % N_DOM
    return jnp.sort(peers, axis=-1).astype(jnp.int32)


def draw_halo_sources(key, part):
    peers = peer_lists(key)
    return peers.astype(jnp.int32)


def draw_block_counts(key, part):
    peers = peer_lists(key)
    listed = (peers[:, :, None] == jnp.arange(N_DOM, dtype=jnp.int32)[None, None, :]).astype(jnp.int32)
    reads = jnp.sum(listed, axis=1)
    return jnp.transpose(reads).astype(jnp.int32)


def draw_tile_sources(key, part):
    key = jax.random.fold_in(key, 11)
    local_key, remote_key = jax.random.split(key)
    own_block = jnp.broadcast_to(jnp.arange(NB, dtype=jnp.int32)[None, :, None], (N_DOM, NB, 1))
    nearby = jax.random.randint(local_key, (N_DOM, NB, 1), 0, NB, dtype=jnp.int32)
    remote_total = NB * (TILES - 2)
    slots = jnp.arange(remote_total, dtype=jnp.int32) % HALO
    scores = jax.random.randint(remote_key, (N_DOM, remote_total), 0, 2 ** 18, dtype=jnp.int32)
    scores = scores * remote_total + jnp.arange(remote_total, dtype=jnp.int32)[None, :]
    shuffle = jnp.argsort(scores, axis=-1, stable=True).astype(jnp.int32)
    remote = NB + jnp.take(slots, shuffle.reshape(-1)).reshape(N_DOM, NB, TILES - 2)
    return jnp.concatenate([own_block, nearby, remote], axis=2).astype(jnp.int32)


def draw_send_rows(key, part):
    key = jax.random.fold_in(key, 23)
    order_key, count_key = jax.random.split(key)
    scores = jax.random.randint(order_key, (N_DOM, N_DOM, ROWS), 0, 2 ** 18, dtype=jnp.int32)
    scores = scores * ROWS + jnp.arange(ROWS, dtype=jnp.int32)
    ordering = jnp.argsort(scores, axis=-1, stable=True)[:, :, :BLOCK].astype(jnp.int32)
    live_count = jax.random.randint(count_key, (N_DOM, N_DOM, 1), 3 * BLOCK // 4, BLOCK + 1, dtype=jnp.int32)
    position = jnp.arange(BLOCK, dtype=jnp.int32)[None, None, :]
    return jnp.where(position < live_count, ordering, ROWS).astype(jnp.int32)


def block_scale(rng, shape, cuts, least, top_value):
    def one(dim, blocks):
        steps = jax.random.uniform(jax.random.fold_in(jax.random.fold_in(rng, 6), dim), (blocks,), jnp.float32, least / len(cuts), top_value / len(cuts))
        return jnp.repeat(jnp.exp(steps), shape[dim] // blocks).reshape((-1,) + (1,) * (len(shape) - dim - 1))

    loudness = one(*cuts[0])
    for cut in cuts[1:]:
        loudness = loudness * one(*cut)
    return loudness


def scatter_about(stream_key, dims, width, limit, pieces=(), kind=jnp.bfloat16):
    result = width * jax.random.normal(stream_key, dims, jnp.float32)
    if pieces:
        result = result * block_scale(stream_key, dims, pieces, -0.22, 0.18)
    return jnp.clip(result, -limit, limit).astype(kind)


def setup_inputs(seed: int = 0) -> dict:
    key_list = jax.random.split(jax.random.key(seed), 10)
    first_layer = scatter_about(key_list[0], (NODES, D), 1.0, 6.0, ((0, 64), (1, 8)))
    w_first = scatter_about(key_list[1], (D, D), D ** -0.5, 0.1875, ((0, 8), (1, 64)))
    w_second = scatter_about(key_list[2], (D, D), D ** -0.5, 0.1875, ((0, 8), (1, 64)))
    tile_values = scatter_about(key_list[3], (N_DOM * NB, TILES, BLOCK, BLOCK), (TILES * BLOCK) ** -0.5, 0.15625, ((0, 64),))
    tile_sources = draw_tile_sources(jax.random.fold_in(key_list[9], 71), 0)
    halo_sources = draw_halo_sources(jax.random.fold_in(key_list[9], 71), 0)
    send_rows = draw_send_rows(jax.random.fold_in(key_list[9], 71), 0)
    block_counts = draw_block_counts(jax.random.fold_in(key_list[9], 71), 0)
    stale_halo = jnp.clip(2.0 * jax.random.uniform(key_list[8], (N_DOM * HALO * BLOCK, D), jnp.float32) ** block_scale(key_list[8], (N_DOM * HALO * BLOCK, D), ((0, 64), (1, 8)), -0.2, 0.2), 0.0, 2.0).astype(jnp.bfloat16)
    return {"first_layer": first_layer, "w_first": w_first, "w_second": w_second, "tile_values": tile_values, "tile_sources": tile_sources, "halo_sources": halo_sources, "send_rows": send_rows, "block_counts": block_counts, "stale_halo": stale_halo}


alpha_mix = 0.1
beta_first = math.log(1.5)
beta_second = math.log(1.25)


def boundary(hidden, send_rows, block_counts, sources, target):
    padded = jnp.concatenate([hidden, jnp.zeros((N_DOM, 1, D), jnp.bfloat16)], axis=1).reshape(N_DOM * (ROWS + 1), D)
    row_list = send_rows[sources, target, :]
    flat_index = (sources[:, None] * (ROWS + 1) + row_list).astype(jnp.int32)
    picked = jnp.take(padded, flat_index.reshape(-1), axis=0).reshape(HALO, BLOCK, D)
    keep_mask = (block_counts[sources, target] > 0)[:, None, None]
    cleared = jnp.where(keep_mask, picked, jnp.zeros_like(picked))
    return cleared.astype(jnp.bfloat16).reshape(HALO * BLOCK, D)


def aggregate(local_rows, halo_rows, tile_blocks, sources):
    all_blocks = jnp.concatenate([local_rows, halo_rows], axis=0).reshape(-1, BLOCK, D)
    chosen = jnp.take(all_blocks, sources.reshape(-1), axis=0).reshape(NB, TILES, BLOCK, D)
    summed = jnp.einsum("ikrc,ikcd->ird", tile_blocks.astype(jnp.float32), chosen.astype(jnp.float32))
    return summed.reshape(ROWS, D)


def grouped_product(rounded, weight):
    share = D // N_FEAT
    left = rounded.reshape(ROWS, N_FEAT, share).astype(jnp.float32)
    right = weight.reshape(N_FEAT, share, D).astype(jnp.float32)
    partial_value = jnp.einsum("rgc,gcd->grd", left, right).astype(jnp.bfloat16)
    return jnp.sum(partial_value.astype(jnp.float32), axis=0)


def layer(local_rows, halo_rows, first_rows, tile_blocks, sources, weight, beta_value):
    aggregated = aggregate(local_rows, halo_rows, tile_blocks, sources)
    mixture = (1.0 - alpha_mix) * aggregated + alpha_mix * first_rows.astype(jnp.float32)
    rounded = mixture.astype(jnp.bfloat16)
    turned = grouped_product(rounded, weight)
    return jax.nn.relu((1.0 - beta_value) * mixture + beta_value * turned).astype(jnp.bfloat16)


def reference(first_layer, w_first, w_second, tile_values, tile_sources, halo_sources, send_rows, block_counts, stale_halo):
    inputs = first_layer.reshape(N_DOM, ROWS, D)
    tile_sets = tile_values.reshape(N_DOM, NB, TILES, BLOCK, BLOCK)
    stale_sets = stale_halo.reshape(N_DOM, HALO * BLOCK, D)
    targets = jnp.arange(N_DOM, dtype=jnp.int32)

    def first_step(operands):
        target, own_rows, tile_blocks, sources, peers = operands
        halo_rows = boundary(inputs, send_rows, block_counts, peers, target)
        return layer(own_rows, halo_rows, own_rows, tile_blocks, sources, w_first, beta_first)

    hidden_one = lax.map(first_step, (targets, inputs, tile_sets, tile_sources, halo_sources))

    def second_step(operands):
        target, own_rows, first_rows, tile_blocks, sources, stale_rows, peers = operands
        output = layer(own_rows, stale_rows, first_rows, tile_blocks, sources, w_second, beta_second)
        return output, boundary(hidden_one, send_rows, block_counts, peers, target)

    layer_out, fresh_halo = lax.map(second_step, (targets, hidden_one, inputs, tile_sets, tile_sources, stale_sets, halo_sources))
    return layer_out.reshape(N_DOM * ROWS, D), fresh_halo.reshape(N_DOM * HALO * BLOCK, D)
```

```python
import math

import jax
import jax.numpy as jnp
from jax import lax
from jax.experimental import pallas as pl
from jax.experimental.pallas import tpu as pltpu
from jax.sharding import PartitionSpec as P

alpha_mix = 0.1
beta_first = math.log(1.5)
beta_second = math.log(1.25)
VMEM_BYTES = 40 * 1024 * 1024
GROUP = 8
bf16 = jnp.bfloat16
f32 = jnp.float32


def params():
    return pltpu.CompilerParams(vmem_limit_bytes=VMEM_BYTES)


def cost(flops, moved):
    return pl.CostEstimate(flops=flops, bytes_accessed=moved, transcendentals=0)


def dot_nt(left, right):
    return lax.dot_general(left, right, (((1,), (1,)), ((), ())), preferred_element_type=f32)


def fold_rows(rows):
    half = rows.shape[0] // 2
    return jnp.concatenate([rows[:half], rows[half:]], axis=1)


def pick_blocks(folded, index_ref, out_ref):
    half = folded.shape[0]
    width = folded.shape[1] // 2
    slots = index_ref.shape[1]
    index = index_ref[0]
    low = index % half
    part = index // half
    lanes = lax.broadcasted_iota(jnp.int32, (slots, half), 1)
    for t in range(index.shape[1]):
        hot = jnp.where(lanes == low[:, t : t + 1], 1.0, 0.0).astype(bf16)
        both = jnp.dot(hot, folded, preferred_element_type=f32)
        side = jnp.broadcast_to(part[:, t : t + 1], (slots, width))
        rows = jnp.where(side == 0, both[:, :width], jnp.where(side == 1, both[:, width:], 0.0))
        out_ref[t] = rows.astype(out_ref.dtype)


def pack_kernel(rows_ref, index_ref, out_ref):
    pick_blocks(fold_rows(rows_ref[...]), index_ref, out_ref)


def pack(rows, index):
    groups, slots, per = index.shape
    count, width = rows.shape
    return pl.pallas_call(
        pack_kernel,
        grid=(groups,),
        in_specs=[
            pl.BlockSpec((count, width), lambda g: (0, 0)),
            pl.BlockSpec((1, slots, per), lambda g: (g, 0, 0)),
        ],
        out_specs=pl.BlockSpec((per, slots, width), lambda g: (g, 0, 0)),
        out_shape=jax.ShapeDtypeStruct((groups * per, slots, width), bf16),
        compiler_params=params(),
        cost_estimate=cost(2 * groups * per * slots * count * width, 3 * 1024 * 1024),
        name="pack",
    )(rows, index)


def layer_kernel(local_tiles, local_ref, first_ref, halo_ref, tiles_ref, weight_ref, sources_ref, peers_ref, part_ref, mixed_ref):
    blocks, tiles = tiles_ref.shape[0], tiles_ref.shape[1]
    size = tiles_ref.shape[2]
    for i in range(blocks):
        total = None
        for k in range(0, tiles, 2):
            pair = []
            for kk in (k, k + 1):
                source = sources_ref[i, kk]
                if kk < local_tiles:
                    start = pl.multiple_of(source * size, size)
                    pair.append(local_ref[pl.ds(start, size), :])
                else:
                    pair.append(halo_ref[peers_ref[source - blocks]])
            left = jnp.concatenate([tiles_ref[i, k], tiles_ref[i, k + 1]], axis=1)
            term = jnp.dot(left, jnp.concatenate(pair, axis=0), preferred_element_type=f32)
            total = term if total is None else total + term
        rows = pl.ds(i * size, size)
        mixed = (1.0 - alpha_mix) * total + alpha_mix * first_ref[rows, :].astype(f32)
        mixed_ref[rows, :] = mixed
    rounded = mixed_ref[...].astype(bf16)
    width = part_ref.shape[2]
    for g in range(part_ref.shape[0]):
        part_ref[g] = dot_nt(rounded, weight_ref[g * width : (g + 1) * width, :]).astype(bf16)


def layer_parts(local_rows, first_rows, halo, tiles, weight, sources, peers, feats, name):
    count, width = local_rows.shape
    vmem = pl.BlockSpec(memory_space=pltpu.VMEM)
    smem = pl.BlockSpec(memory_space=pltpu.SMEM)

    def kernel(*refs):
        layer_kernel(2, *refs)

    return pl.pallas_call(
        kernel,
        in_specs=[vmem] * 5 + [smem] * 2,
        out_specs=[vmem] * 2,
        out_shape=[
            jax.ShapeDtypeStruct((feats, count, width), bf16),
            jax.ShapeDtypeStruct((count, width), f32),
        ],
        compiler_params=params(),
        cost_estimate=cost(300 * 1000 * 1000, 6 * 1024 * 1024),
        name=name,
    )(local_rows, first_rows, halo, tiles, weight, sources, peers)


def finished(beta, part_ref, mixed_ref):
    turned = part_ref[0].astype(f32)
    for g in range(1, part_ref.shape[0]):
        turned = turned + part_ref[g].astype(f32)
    return jax.nn.relu((1.0 - beta) * mixed_ref[...] + beta * turned).astype(bf16)


def hidden_pack_kernel(part_ref, mixed_ref, index_ref, out_ref, hidden_ref, folded_ref):
    @pl.when(pl.program_id(0) == 0)
    def _():
        hidden = finished(beta_first, part_ref, mixed_ref)
        hidden_ref[...] = hidden
        folded_ref[...] = fold_rows(hidden)

    pick_blocks(folded_ref[...], index_ref, out_ref)


def hidden_pack(parts, mixed, index):
    groups, slots, per = index.shape
    feats, count, width = parts.shape
    return pl.pallas_call(
        hidden_pack_kernel,
        grid=(groups,),
        in_specs=[
            pl.BlockSpec((feats, count, width), lambda g: (0, 0, 0)),
            pl.BlockSpec((count, width), lambda g: (0, 0)),
            pl.BlockSpec((1, slots, per), lambda g: (g, 0, 0)),
        ],
        out_specs=[
            pl.BlockSpec((per, slots, width), lambda g: (g, 0, 0)),
            pl.BlockSpec((count, width), lambda g: (0, 0)),
        ],
        out_shape=[
            jax.ShapeDtypeStruct((groups * per, slots, width), bf16),
            jax.ShapeDtypeStruct((count, width), bf16),
        ],
        scratch_shapes=[pltpu.VMEM((count // 2, 2 * width), bf16)],
        compiler_params=params(),
        cost_estimate=cost(2 * groups * per * slots * count * width, 4 * 1024 * 1024),
        name="hidden_pack",
    )(parts, mixed, index)


def final_kernel(part_ref, mixed_ref, out_ref):
    out_ref[...] = finished(beta_second, part_ref, mixed_ref)


def final_rows(parts, mixed):
    vmem = pl.BlockSpec(memory_space=pltpu.VMEM)
    return pl.pallas_call(
        final_kernel,
        in_specs=[vmem] * 2,
        out_specs=vmem,
        out_shape=jax.ShapeDtypeStruct(mixed.shape, bf16),
        compiler_params=params(),
        cost_estimate=cost(1000 * 1000, 2 * 1024 * 1024),
        name="final_rows",
    )(parts, mixed)


def compact_kernel(peers_ref, arrived_ref, out_ref, sems):
    copies = [
        pltpu.make_async_copy(arrived_ref.at[peers_ref[j]], out_ref.at[j], sems.at[j])
        for j in range(out_ref.shape[0])
    ]
    for copy in copies:
        copy.start()
    for copy in copies:
        copy.wait()


def compact(arrived, peers):
    shape = (peers.shape[0],) + arrived.shape[1:]
    out = pl.pallas_call(
        compact_kernel,
        in_specs=[pl.BlockSpec(memory_space=pltpu.SMEM), pl.BlockSpec(memory_space=pl.ANY)],
        out_specs=pl.BlockSpec(memory_space=pl.ANY),
        out_shape=jax.ShapeDtypeStruct(shape, arrived.dtype),
        scratch_shapes=[pltpu.SemaphoreType.DMA((shape[0],))],
        cost_estimate=cost(0, 2 * 1024 * 1024),
        name="compact",
    )(peers, arrived)
    return out.reshape(-1, arrived.shape[2])


def spread(weight, peers):
    turned = weight.T
    sent = jnp.broadcast_to(turned[None], (peers,) + turned.shape)
    got = lax.all_to_all(sent, "dom", split_axis=0, concat_axis=0, tiled=True)
    return got.reshape(-1, turned.shape[1])


def swap(blocks, axis):
    return lax.all_to_all(blocks, axis, split_axis=0, concat_axis=0, tiled=True)


def shards(
    first_layer,
    w_first,
    w_second,
    tile_values,
    tile_sources,
    halo_sources,
    send_rows,
    block_counts,
    stale_halo,
):
    count, width = first_layer.shape
    peers, slots = send_rows.shape[1:]
    feats = lax.axis_size("feat")
    halos = halo_sources.shape[1]
    sources = tile_sources[0]
    listed = halo_sources[0]
    index = jnp.where((block_counts[0] > 0)[:, None], send_rows[0], count)
    index = index.reshape(-1, GROUP, slots).transpose(0, 2, 1)

    first_weight = spread(w_first, peers)
    arrived = swap(pack(first_layer, index), "dom")
    parts, mixed = layer_parts(
        first_layer, first_layer, arrived, tile_values, first_weight, sources, listed, feats, "layer_first"
    )
    parts, w_second = lax.optimization_barrier((parts, w_second))
    second_weight = spread(w_second, peers)
    got = swap(parts, "feat")
    sending, hidden = hidden_pack(got, mixed, index)
    received = swap(sending, "dom")
    stale = stale_halo.reshape(halos, slots, width)
    order = jnp.arange(halos, dtype=jnp.int32)
    parts_two, mixed_two = layer_parts(
        hidden, first_layer, stale, tile_values, second_weight, sources, order, feats, "layer_second"
    )
    got_two = swap(parts_two, "feat")
    layer_out = final_rows(got_two, mixed_two)
    fresh_halo = compact(received, listed)
    return (layer_out, fresh_halo)


def solution(mesh):
    placed = (
        P("dom", "feat"),
        P("feat", "dom"),
        P("feat", "dom"),
        P("dom", None, None, None),
        P("dom", None, None),
        P("dom", None),
        P("dom", None, None),
        P("dom", None),
        P("dom", "feat"),
    )
    return jax.shard_map(
        shards,
        mesh=mesh,
        in_specs=placed,
        out_specs=(P("dom", "feat"), P("dom", "feat")),
        check_vma=False,
    )
```

```python
import math

import jax
import jax.numpy as jnp
from jax import lax
from jax.experimental import pallas as pl
from jax.experimental.pallas import tpu as pltpu
from jax.sharding import PartitionSpec as P

alpha_mix = 0.1
beta_first = math.log(1.5)
beta_second = math.log(1.25)
VMEM_BYTES = 16 * 1024 * 1024
GROUP = 8
RANKS = 8
bf16 = jnp.bfloat16
f32 = jnp.float32
i32 = jnp.int32
vmem = pl.BlockSpec(memory_space=pltpu.VMEM)
smem = pl.BlockSpec(memory_space=pltpu.SMEM)


def params(limit=VMEM_BYTES):
    return pltpu.CompilerParams(vmem_limit_bytes=limit)


def cost(flops, moved):
    return pl.CostEstimate(flops=flops, bytes_accessed=moved, transcendentals=0)


def in_hbm(*arrays):
    return [pltpu.with_memory_space_constraint(array, pltpu.HBM) for array in arrays]


def dot_nt(left, right):
    return lax.dot_general(left, right, (((1,), (1,)), ((), ())), preferred_element_type=f32)


def fold_rows(rows):
    half = rows.shape[0] // 2
    return jnp.concatenate([rows[:half], rows[half:]], axis=1)


def prepare_index(rows_ref, counts_ref, half, low_ref, high_ref):
    lanes = rows_ref.shape[1]
    copies = lanes // rows_ref.shape[0]
    index = jnp.concatenate([rows_ref[...]] * copies, axis=0).T
    counts = jnp.concatenate([counts_ref[...]] * copies, axis=1)
    high = index >= half
    live = jnp.logical_and(counts > 0, index < 2 * half)
    low = jnp.where(live, index - jnp.where(high, half, 0), half + 44)
    low_ref[...] = low.astype(f32)
    high_ref[...] = jnp.where(high, 1.0, 0.0)


def pick_blocks(folded, low, high, blocks_ref, out_ref, sems):
    half = folded.shape[0]
    width = folded.shape[1] // 2
    targets, slots = blocks_ref.shape[0], blocks_ref.shape[1]
    lanes = low.shape[1]
    places = [
        (lax.broadcasted_iota(i32, (slots, lanes), 1) + first).astype(f32).astype(bf16)
        for first in range(0, half, lanes)
    ]
    one, zero = jnp.ones((slots, lanes), bf16), jnp.zeros((slots, lanes), bf16)
    copies = []
    for t in range(targets):
        wanted = jnp.broadcast_to(low[:, t : t + 1], (slots, lanes)).astype(bf16)
        hot = jnp.concatenate([jnp.where(wanted == place, one, zero) for place in places], axis=1)
        both = jnp.dot(hot, folded, preferred_element_type=f32)
        side = jnp.broadcast_to(high[:, t : t + 1], (slots, width))
        blocks_ref[t] = jnp.where(side > 0.5, both[:, width:], both[:, :width]).astype(bf16)
        if (t + 1) % GROUP == 0:
            span = pl.ds(t + 1 - GROUP, GROUP)
            copy = pltpu.make_async_copy(blocks_ref.at[span], out_ref.at[span], sems.at[t // GROUP])
            copy.start()
            copies.append(copy)
    return copies


def pack_kernel(rows_ref, picks_ref, counts_ref, out_ref, blocks_ref, low_ref, high_ref, sems):
    prepare_index(picks_ref, counts_ref, rows_ref.shape[0] // 2, low_ref, high_ref)
    copies = pick_blocks(fold_rows(rows_ref[...]), low_ref[...], high_ref[...], blocks_ref, out_ref, sems)
    for copy in copies:
        copy.wait()


def pack(rows, picks, counts):
    targets, slots = picks.shape
    count, width = rows.shape
    return pl.pallas_call(
        pack_kernel,
        in_specs=[vmem] * 3,
        out_specs=pl.BlockSpec(memory_space=pltpu.HBM),
        out_shape=pltpu.HBM((targets, slots, width), bf16),
        scratch_shapes=[
            pltpu.VMEM((targets, slots, width), bf16),
            pltpu.VMEM((slots, slots), f32),
            pltpu.VMEM((slots, slots), f32),
            pltpu.SemaphoreType.DMA((targets // GROUP,)),
        ],
        compiler_params=params(),
        cost_estimate=cost(2 * targets * slots * count * width, 3 * 1024 * 1024),
        name="pack",
    )(*in_hbm(rows, picks, counts))


def tile_pairs(tiles_ref, i, firsts, block):
    total = None
    for k in firsts:
        left = jnp.concatenate([tiles_ref[i, k], tiles_ref[i, k + 1]], axis=1)
        right = jnp.concatenate([block(i, k), block(i, k + 1)], axis=0)
        term = jnp.dot(left, right, preferred_element_type=f32)
        total = term if total is None else total + term
    return total


def local_sum(tiles_ref, sources_ref, local_ref, i):
    size = tiles_ref.shape[2]

    def block(i, k):
        return local_ref[pl.ds(pl.multiple_of(sources_ref[i, k] * size, size), size), :]

    return tile_pairs(tiles_ref, i, [0], block)


def halo_sum(tiles_ref, sources_ref, block_of, i):
    blocks, tiles = tiles_ref.shape[0], tiles_ref.shape[1]

    def block(i, k):
        return block_of(sources_ref[i, k] - blocks)

    return tile_pairs(tiles_ref, i, range(2, tiles, 2), block)


def first_kernel(local_ref, halo_ref, tiles_ref, sources_ref, peers_ref, out_ref, mixed_ref, rounded_ref, sems):
    size = tiles_ref.shape[2]
    for i in range(tiles_ref.shape[0]):
        total = local_sum(tiles_ref, sources_ref, local_ref, i)
        total = total + halo_sum(tiles_ref, sources_ref, lambda j: halo_ref[peers_ref[j]], i)
        rows = pl.ds(i * size, size)
        mixed = (1.0 - alpha_mix) * total + alpha_mix * local_ref[rows, :].astype(f32)
        mixed_ref[rows, :] = mixed
        rounded_ref[rows, :] = mixed.astype(bf16)
    copies = [
        pltpu.make_async_copy(rounded_ref, out_ref.at[g], sems.at[g]) for g in range(out_ref.shape[0])
    ]
    for copy in copies:
        copy.start()
    for copy in copies:
        copy.wait()


def first_mixture(rows, halo, tiles, sources, peers, copies):
    count, width = rows.shape
    return pl.pallas_call(
        first_kernel,
        in_specs=[vmem] * 3 + [smem] * 2,
        out_specs=[pl.BlockSpec(memory_space=pltpu.HBM), vmem],
        out_shape=[
            pltpu.HBM((copies, count, width), bf16),
            jax.ShapeDtypeStruct((count, width), f32),
        ],
        scratch_shapes=[pltpu.VMEM((count, width), bf16), pltpu.SemaphoreType.DMA((copies,))],
        compiler_params=params(),
        cost_estimate=cost(170 * 1000 * 1000, 5 * 1024 * 1024),
        name="first_mixture",
    )(rows, halo, tiles, sources, peers)


def stale_kernel(first_ref, stale_ref, tiles_ref, sources_ref, out_ref):
    size = tiles_ref.shape[2]
    for i in range(tiles_ref.shape[0]):
        total = halo_sum(tiles_ref, sources_ref, lambda j: stale_ref[j], i)
        rows = pl.ds(i * size, size)
        out_ref[rows, :] = (1.0 - alpha_mix) * total + alpha_mix * first_ref[rows, :].astype(f32)


def stale_mixture(first_rows, stale, tiles, sources):
    return pl.pallas_call(
        stale_kernel,
        in_specs=[vmem] * 3 + [smem],
        out_specs=vmem,
        out_shape=jax.ShapeDtypeStruct(first_rows.shape, f32),
        compiler_params=params(),
        cost_estimate=cost(140 * 1000 * 1000, 4 * 1024 * 1024),
        name="stale_mixture",
    )(first_rows, stale, tiles, sources)


def columns_of(weight_ref, layer):
    half = weight_ref.shape[1] // 2
    return lambda z: weight_ref[z, pl.ds(layer * half, half), :]


def finished(beta, parts, mixed, weight_of):
    turned = None
    for (z, first), (zz, second) in zip(parts[::2], parts[1::2]):
        left = jnp.concatenate([first[...], second[...]], axis=1)
        right = jnp.concatenate([weight_of(z), weight_of(zz)], axis=1)
        term = dot_nt(left, right)
        turned = term if turned is None else turned + term
    return jax.nn.relu((1.0 - beta) * mixed + beta * turned).astype(bf16)


def hidden_kernel(
    parts_ref,
    mixed_ref,
    weight_ref,
    stale_ref,
    tiles_ref,
    picks_ref,
    counts_ref,
    sources_ref,
    out_ref,
    rounded_ref,
    second_ref,
    blocks_ref,
    hidden_ref,
    low_ref,
    high_ref,
    sems,
):
    prepare_index(picks_ref, counts_ref, mixed_ref.shape[0] // 2, low_ref, high_ref)
    parts = [(z, parts_ref.at[z]) for z in range(parts_ref.shape[0])]
    hidden = finished(beta_first, parts, mixed_ref[...], columns_of(weight_ref, 0))
    hidden_ref[...] = hidden
    copies = pick_blocks(fold_rows(hidden), low_ref[...], high_ref[...], blocks_ref, out_ref, sems)
    size = tiles_ref.shape[2]
    for i in range(tiles_ref.shape[0]):
        rows = pl.ds(i * size, size)
        total = local_sum(tiles_ref, sources_ref, hidden_ref, i)
        mixed = (1.0 - alpha_mix) * total + stale_ref[rows, :]
        second_ref[rows, :] = mixed
        rounded_ref[rows, :] = mixed.astype(bf16)
    for copy in copies:
        copy.wait()


def hidden_pack(parts, mixed, weights, stale_mixed, tiles, picks, counts, sources):
    targets, slots = picks.shape
    feats, count, width = parts.shape

    def part(array, *shape):
        return pl.BlockSpec(shape or array.shape, lambda g: (0,) * array.ndim)

    return pl.pallas_call(
        hidden_kernel,
        grid=(1,),
        in_specs=[
            part(parts),
            part(mixed),
            part(weights),
            part(stale_mixed),
            part(tiles, tiles.shape[0], 2, *tiles.shape[2:]),
            part(picks),
            part(counts),
            smem,
        ],
        out_specs=[
            pl.BlockSpec(memory_space=pltpu.HBM),
            pl.BlockSpec((count, width), lambda g: (0, 0)),
            pl.BlockSpec((count, width), lambda g: (0, 0)),
        ],
        out_shape=[
            pltpu.HBM((targets, slots, width), bf16),
            pltpu.HBM((count, width), bf16),
            pltpu.HBM((count, width), f32),
        ],
        scratch_shapes=[
            pltpu.VMEM((targets, slots, width), bf16),
            pltpu.VMEM((count, width), bf16),
            pltpu.VMEM((slots, slots), f32),
            pltpu.VMEM((slots, slots), f32),
            pltpu.SemaphoreType.DMA((targets // GROUP,)),
        ],
        compiler_params=params(),
        cost_estimate=cost(2 * targets * slots * count * width, 6 * 1024 * 1024),
        name="hidden_pack",
    )(parts, *in_hbm(mixed), weights, *in_hbm(stale_mixed, tiles, picks, counts), sources)


def final_kernel(place_ref, mixed_ref, weight_ref, *refs):
    feats = weight_ref.shape[0]
    parts = [(lax.rem(place_ref[0] + feats - k, feats), refs[k]) for k in range(feats)]
    refs[-1][...] = finished(beta_second, parts, mixed_ref[...], columns_of(weight_ref, 1))


def final_rows(place, mixed, weights, parts):
    return pl.pallas_call(
        final_kernel,
        in_specs=[smem] + [vmem] * (2 + len(parts)),
        out_specs=vmem,
        out_shape=jax.ShapeDtypeStruct(mixed.shape, bf16),
        compiler_params=params(),
        cost_estimate=cost(134 * 1000 * 1000, 3 * 1024 * 1024),
        name="final_rows",
    )(place, mixed, weights, *parts)


def compact_kernel(peers_ref, arrived_ref, out_ref, sems):
    copies = [
        pltpu.make_async_copy(arrived_ref.at[peers_ref[j]], out_ref.at[j], sems.at[j])
        for j in range(out_ref.shape[0])
    ]
    for copy in copies:
        copy.start()
    for copy in copies:
        copy.wait()


def compact(arrived, peers):
    shape = (peers.shape[0],) + arrived.shape[1:]
    out = pl.pallas_call(
        compact_kernel,
        in_specs=[smem, vmem],
        out_specs=pl.BlockSpec(memory_space=pl.ANY),
        out_shape=jax.ShapeDtypeStruct(shape, arrived.dtype),
        scratch_shapes=[pltpu.SemaphoreType.DMA((shape[0],))],
        compiler_params=params(16 * 1024 * 1024),
        cost_estimate=cost(0, 2 * 1024 * 1024),
        name="compact",
    )(peers, arrived)
    return out.reshape(-1, arrived.shape[2])


def slab_columns(w_first, w_second, feats):
    both = jnp.concatenate([w_first.T, w_second.T], axis=0)
    pairs = [
        ((z * RANKS + r) * feats + y, (y * RANKS + r) * feats + z)
        for z in range(feats)
        for r in range(RANKS)
        for y in range(feats)
    ]
    both = lax.ppermute(both, ("dom", "feat"), pairs)
    slabs = [[z * RANKS + r for r in range(RANKS)] for z in range(feats)]
    got = lax.all_gather(both, "dom", axis=0, tiled=True, axis_index_groups=slabs)
    return got.reshape(RANKS, 2, -1, both.shape[1]).swapaxes(0, 1).reshape(got.shape)


def own_columns(rows, feats):
    columns = [[z * RANKS + r for z in range(feats)] for r in range(RANKS)]
    return lax.all_gather(rows, "dom", axis=0, tiled=False, axis_index_groups=columns)


def around(rows, axis):
    size = lax.axis_size(axis)
    return [rows] + [
        lax.ppermute(rows, axis, [(i, (i + k) % size) for i in range(size)]) for k in range(1, size)
    ]


def swap(blocks, axis):
    return lax.all_to_all(blocks, axis, split_axis=0, concat_axis=0, tiled=True)


def shards(
    first_layer,
    w_first,
    w_second,
    tile_values,
    tile_sources,
    halo_sources,
    send_rows,
    block_counts,
    stale_halo,
):
    picks = send_rows[0]
    feats = lax.axis_size("feat")
    sources = tile_sources[0]
    listed = halo_sources[0]
    stale = stale_halo.reshape(listed.shape[0], picks.shape[1], -1)

    leaving = pack(first_layer, picks, block_counts)
    leaving, w_first, w_second = lax.optimization_barrier((leaving, w_first, w_second))
    slab = slab_columns(w_first, w_second, feats)
    arrived = swap(leaving, "dom")
    stale_mixed = stale_mixture(first_layer, stale, tile_values, sources)
    rounded, mixed = first_mixture(first_layer, arrived, tile_values, sources, listed, feats)
    rounded, slab = lax.optimization_barrier((rounded, slab))
    parts = swap(rounded, "feat")
    weights = own_columns(slab, feats)
    sending, rounded_two, mixed_two = hidden_pack(
        parts, mixed, weights, stale_mixed, tile_values, picks, block_counts, sources
    )
    received = swap(sending, "dom")
    place = lax.axis_index("feat").astype(i32).reshape(1)
    layer_out = final_rows(place, mixed_two, weights, around(rounded_two, "feat"))
    fresh_halo = compact(received, listed)
    return (layer_out, fresh_halo)


def solution(mesh):
    placed = (
        P("dom", "feat"),
        P("feat", "dom"),
        P("feat", "dom"),
        P("dom", None, None, None),
        P("dom", None, None),
        P("dom", None),
        P("dom", None, None),
        P("dom", None),
        P("dom", "feat"),
    )
    return jax.shard_map(
        shards,
        mesh=mesh,
        in_specs=placed,
        out_specs=(P("dom", "feat"), P("dom", "feat")),
        check_vma=False,
    )
```

```python
import math

import jax
import jax.numpy as jnp
from jax import lax
from jax.experimental import pallas as pl
from jax.experimental.pallas import tpu as pltpu
from jax.sharding import PartitionSpec as P

alpha_mix = 0.1
beta_first = math.log(1.5)
beta_second = math.log(1.25)
VMEM_BYTES = 16 * 1024 * 1024
RANKS = 8
SEND = 8
GROUP = 2
bf16 = jnp.bfloat16
f32 = jnp.float32
i32 = jnp.int32
vmem = pl.BlockSpec(memory_space=pltpu.VMEM)
smem = pl.BlockSpec(memory_space=pltpu.SMEM)


def params(limit=VMEM_BYTES):
    return pltpu.CompilerParams(vmem_limit_bytes=limit)


def cost(flops, moved):
    return pl.CostEstimate(flops=flops, bytes_accessed=moved, transcendentals=0)


def in_hbm(*arrays):
    return [pltpu.with_memory_space_constraint(array, pltpu.HBM) for array in arrays]


def dot_nt(left, right):
    return lax.dot_general(left, right, (((1,), (1,)), ((), ())), preferred_element_type=f32)


def fold_rows(rows):
    half = rows.shape[0] // 2
    return jnp.concatenate([rows[:half], rows[half:]], axis=1)


def place_of(picks, counts, half):
    targets = picks.shape[0]
    square = (targets, targets)
    same = lax.broadcasted_iota(i32, square, 0) == lax.broadcasted_iota(i32, square, 1)
    listed = jnp.where(same, jnp.broadcast_to(counts, square), 0)
    listed = jnp.sum(listed, axis=1, keepdims=True)
    high = picks >= half
    live = jnp.logical_and(listed > 0, picks < 2 * half)
    low = jnp.where(live, picks - jnp.where(high, half, 0), half + 44)
    return low.astype(f32), jnp.where(high, 1.0, 0.0)


def turned(rows):
    return jnp.concatenate([rows] * (rows.shape[1] // rows.shape[0]), axis=0).T


def picker(half, slots, width):
    lanes = slots
    places = [
        (lax.broadcasted_iota(i32, (slots, lanes), 1) + first).astype(f32).astype(bf16)
        for first in range(0, half, lanes)
    ]
    one, zero = jnp.ones((slots, lanes), bf16), jnp.zeros((slots, lanes), bf16)

    def pick(folded, low, high):
        wanted = jnp.broadcast_to(low, (slots, lanes)).astype(bf16)
        hot = jnp.concatenate([jnp.where(wanted == place, one, zero) for place in places], axis=1)
        both = jnp.dot(hot, folded, preferred_element_type=f32)
        side = jnp.broadcast_to(high, (slots, width))
        return jnp.where(side > 0.5, both[:, width:], both[:, :width]).astype(bf16)

    return pick


def pack_first_kernel(rows_ref, picks_ref, counts_ref, out_ref, index_ref, blocks_ref, places_ref, sems):
    targets, slots, width = blocks_ref.shape
    groups = index_ref.shape[0]
    half = rows_ref.shape[0] // 2
    low, high = place_of(picks_ref[...], counts_ref[...], half)
    per = targets // groups
    for g in range(groups):
        places_ref[g, 0:per, :] = low[g * per : (g + 1) * per].astype(bf16)
        places_ref[g, per : 2 * per, :] = high[g * per : (g + 1) * per].astype(bf16)
    copies = [pltpu.make_async_copy(places_ref, index_ref, sems.at[targets // SEND])]
    copies[0].start()
    low, high = turned(low), turned(high)
    folded = fold_rows(rows_ref[...])
    pick = picker(half, slots, width)
    for t in range(targets):
        blocks_ref[t] = pick(folded, low[:, t : t + 1], high[:, t : t + 1])
        if (t + 1) % SEND == 0:
            span = pl.ds(t + 1 - SEND, SEND)
            copies.append(pltpu.make_async_copy(blocks_ref.at[span], out_ref.at[span], sems.at[t // SEND]))
            copies[-1].start()
    for copy in copies:
        copy.wait()


def pack_first(rows, picks, counts, groups):
    targets, slots = picks.shape
    count, width = rows.shape
    index = (groups, 2 * targets // groups, slots)
    return pl.pallas_call(
        pack_first_kernel,
        in_specs=[vmem] * 3,
        out_specs=[pl.BlockSpec(memory_space=pltpu.HBM)] * 2,
        out_shape=[pltpu.HBM((targets, slots, width), bf16), pltpu.HBM(index, bf16)],
        scratch_shapes=[
            pltpu.VMEM((targets, slots, width), bf16),
            pltpu.VMEM(index, bf16),
            pltpu.SemaphoreType.DMA((targets // SEND + 1,)),
        ],
        compiler_params=params(),
        cost_estimate=cost(2 * targets * slots * count * width, 3 * 1024 * 1024),
        name="pack_first",
    )(*in_hbm(rows, picks, counts))


def pack_second_kernel(group_ref, rows_ref, *refs):
    groups = rows_ref.shape[0]
    index_refs, (out_ref, blocks_ref, sems) = refs[:groups], refs[groups:]
    targets, _, slots, width = blocks_ref.shape
    half = rows_ref.shape[1] // 2
    own = group_ref[0]
    places = [ref[own].astype(f32) for ref in index_refs]
    low = turned(jnp.concatenate([place[:targets] for place in places], axis=0))
    high = turned(jnp.concatenate([place[targets:] for place in places], axis=0))
    sources = [lax.rem(own + groups - k, groups) for k in range(groups)]
    folded = [fold_rows(rows_ref[source]) for source in sources]
    pick = picker(half, slots, width)
    copies = []
    for t in range(targets):
        for k in range(groups):
            c = k * targets + t
            blocks_ref[t, sources[k]] = pick(folded[k], low[:, c : c + 1], high[:, c : c + 1])
        if (t + 1) % GROUP == 0:
            span = pl.ds(t + 1 - GROUP, GROUP)
            copies.append(pltpu.make_async_copy(blocks_ref.at[span], out_ref.at[span], sems.at[t // GROUP]))
            copies[-1].start()
    for copy in copies:
        copy.wait()


def pack_second(group, rows, index, targets):
    groups, count, width = rows.shape
    shape = (targets, groups, width, width)
    return pl.pallas_call(
        pack_second_kernel,
        in_specs=[smem] + [vmem] * (1 + groups),
        out_specs=pl.BlockSpec(memory_space=pltpu.HBM),
        out_shape=pltpu.HBM(shape, bf16),
        scratch_shapes=[pltpu.VMEM(shape, bf16), pltpu.SemaphoreType.DMA((shape[0] // GROUP,))],
        compiler_params=params(),
        cost_estimate=cost(2 * shape[0] * groups * width * count * width, 3 * 1024 * 1024),
        name="pack_second",
    )(group, rows, *index)


def arrival(source, ranks, groups):
    return lax.rem(source, ranks) * groups + lax.div(source, ranks)


def tile_pairs(tiles_ref, i, firsts, block):
    total = None
    for k in firsts:
        left = jnp.concatenate([tiles_ref[i, k], tiles_ref[i, k + 1]], axis=1)
        right = jnp.concatenate([block(i, k), block(i, k + 1)], axis=0)
        term = jnp.dot(left, right, preferred_element_type=f32)
        total = term if total is None else total + term
    return total


def local_sum(tiles_ref, sources_ref, local_ref, i):
    size = tiles_ref.shape[2]

    def block(i, k):
        return local_ref[pl.ds(pl.multiple_of(sources_ref[i, k] * size, size), size), :]

    return tile_pairs(tiles_ref, i, [0], block)


def halo_sum(tiles_ref, sources_ref, block_of, i):
    blocks, tiles = tiles_ref.shape[0], tiles_ref.shape[1]

    def block(i, k):
        return block_of(sources_ref[i, k] - blocks)

    return tile_pairs(tiles_ref, i, range(2, tiles, 2), block)


def first_kernel(local_ref, halo_ref, tiles_ref, sources_ref, peers_ref, out_ref, rounded_ref, sems):
    size = tiles_ref.shape[2]
    for i in range(tiles_ref.shape[0]):
        total = local_sum(tiles_ref, sources_ref, local_ref, i)
        total = total + halo_sum(tiles_ref, sources_ref, lambda j: halo_ref[peers_ref[j]], i)
        rows = pl.ds(i * size, size)
        mixed = (1.0 - alpha_mix) * total + alpha_mix * local_ref[rows, :].astype(f32)
        rounded_ref[rows, :] = mixed.astype(bf16)
    copies = [
        pltpu.make_async_copy(rounded_ref, out_ref.at[g], sems.at[g]) for g in range(out_ref.shape[0])
    ]
    for copy in copies:
        copy.start()
    for copy in copies:
        copy.wait()


def first_mixture(rows, halo, tiles, sources, peers, copies):
    count, width = rows.shape
    return pl.pallas_call(
        first_kernel,
        in_specs=[vmem] * 3 + [smem] * 2,
        out_specs=pl.BlockSpec(memory_space=pltpu.HBM),
        out_shape=pltpu.HBM((copies, count, width), bf16),
        scratch_shapes=[pltpu.VMEM((count, width), bf16), pltpu.SemaphoreType.DMA((copies,))],
        compiler_params=params(),
        cost_estimate=cost(170 * 1000 * 1000, 5 * 1024 * 1024),
        name="first_mixture",
    )(rows, halo, tiles, sources, peers)


def stale_kernel(first_ref, stale_ref, tiles_ref, sources_ref, out_ref):
    size = tiles_ref.shape[2]
    for i in range(tiles_ref.shape[0]):
        total = halo_sum(tiles_ref, sources_ref, lambda j: stale_ref[j], i)
        rows = pl.ds(i * size, size)
        out_ref[rows, :] = (1.0 - alpha_mix) * total + alpha_mix * first_ref[rows, :].astype(f32)


def stale_mixture(first_rows, stale, tiles, sources):
    return pl.pallas_call(
        stale_kernel,
        in_specs=[vmem] * 3 + [smem],
        out_specs=vmem,
        out_shape=pltpu.HBM(first_rows.shape, f32),
        compiler_params=params(),
        cost_estimate=cost(140 * 1000 * 1000, 4 * 1024 * 1024),
        name="stale_mixture",
    )(first_rows, stale, tiles, sources)


def second_kernel(hidden_ref, stale_ref, tiles_ref, sources_ref, rounded_ref):
    size = tiles_ref.shape[2]
    for i in range(tiles_ref.shape[0]):
        rows = pl.ds(i * size, size)
        total = local_sum(tiles_ref, sources_ref, hidden_ref.at[0], i)
        rounded_ref[rows, :] = ((1.0 - alpha_mix) * total + stale_ref[rows, :]).astype(bf16)


def second_mixture(hidden_copies, stale_mixed, tiles, sources):
    shape = stale_mixed.shape
    return pl.pallas_call(
        second_kernel,
        grid=(1,),
        in_specs=[
            pl.BlockSpec((1,) + shape, lambda g: (0, 0, 0)),
            pl.BlockSpec(shape, lambda g: (0, 0)),
            pl.BlockSpec((tiles.shape[0], 2) + tiles.shape[2:], lambda g: (0, 0, 0, 0)),
            smem,
        ],
        out_specs=pl.BlockSpec(shape, lambda g: (0, 0)),
        out_shape=jax.ShapeDtypeStruct(shape, bf16),
        compiler_params=params(),
        cost_estimate=cost(34 * 1000 * 1000, 2 * 1024 * 1024),
        name="second_mixture",
    )(*in_hbm(hidden_copies, stale_mixed, tiles), sources)


def columns_of(weight_ref, layer):
    half = weight_ref.shape[1] // 2
    return lambda z: weight_ref[z, pl.ds(layer * half, half), :]


def finished(beta, parts, own, weight_of):
    turned = None
    for (z, first), (zz, second) in zip(parts[::2], parts[1::2]):
        left = jnp.concatenate([first, second], axis=1)
        right = jnp.concatenate([weight_of(z), weight_of(zz)], axis=1)
        term = dot_nt(left, right)
        turned = term if turned is None else turned + term
    return jax.nn.relu((1.0 - beta) * own.astype(f32) + beta * turned).astype(bf16)


def hidden_kernel(place_ref, parts_ref, weight_ref, out_ref, hidden_ref, sems):
    parts = [(z, parts_ref[z]) for z in range(parts_ref.shape[0])]
    hidden_ref[...] = finished(beta_first, parts, parts_ref[place_ref[0]], columns_of(weight_ref, 0))
    copies = [
        pltpu.make_async_copy(hidden_ref, out_ref.at[g], sems.at[g]) for g in range(out_ref.shape[0])
    ]
    for copy in copies:
        copy.start()
    for copy in copies:
        copy.wait()


def hidden_copies(place, parts, weights, groups):
    shape = parts.shape[1:]
    return pl.pallas_call(
        hidden_kernel,
        in_specs=[smem] + [vmem] * 2,
        out_specs=pl.BlockSpec(memory_space=pltpu.HBM),
        out_shape=pltpu.HBM((groups,) + shape, bf16),
        scratch_shapes=[pltpu.VMEM(shape, bf16), pltpu.SemaphoreType.DMA((groups,))],
        compiler_params=params(),
        cost_estimate=cost(134 * 1000 * 1000, 3 * 1024 * 1024),
        name="hidden",
    )(place, parts, weights)


def final_kernel(places, place_ref, weight_ref, *refs):
    feats = len(places)
    parts = [(lax.rem(place_ref[0] + (feats - k), feats), ref[...]) for k, ref in zip(places, refs)]
    refs[-1][...] = finished(beta_second, parts, refs[0][...], columns_of(weight_ref, 1))


def final_rows(place, weights, parts):
    places = list(parts)

    def kernel(*refs):
        final_kernel(places, *refs)

    return pl.pallas_call(
        kernel,
        in_specs=[smem] + [vmem] * (1 + len(parts)),
        out_specs=vmem,
        out_shape=jax.ShapeDtypeStruct(parts[0].shape, bf16),
        compiler_params=params(),
        cost_estimate=cost(134 * 1000 * 1000, 3 * 1024 * 1024),
        name="final_rows",
    )(place, weights, *parts.values())


def compact_kernel(groups, peers_ref, arrived_ref, out_ref, sems):
    ranks = arrived_ref.shape[0] // groups
    copies = [
        pltpu.make_async_copy(
            arrived_ref.at[arrival(peers_ref[j], ranks, groups)], out_ref.at[j], sems.at[j]
        )
        for j in range(out_ref.shape[0])
    ]
    for copy in copies:
        copy.start()
    for copy in copies:
        copy.wait()


def compact(arrived, peers, groups):
    shape = (peers.shape[0],) + arrived.shape[1:]

    def kernel(*refs):
        compact_kernel(groups, *refs)

    out = pl.pallas_call(
        kernel,
        in_specs=[smem, vmem],
        out_specs=pl.BlockSpec(memory_space=pl.ANY),
        out_shape=jax.ShapeDtypeStruct(shape, arrived.dtype),
        scratch_shapes=[pltpu.SemaphoreType.DMA((shape[0],))],
        compiler_params=params(),
        cost_estimate=cost(0, 2 * 1024 * 1024),
        name="compact",
    )(peers, arrived)
    return out.reshape(-1, arrived.shape[2])


def slab_columns(w_first, w_second, feats):
    both = jnp.concatenate([w_first.T, w_second.T], axis=0)
    pairs = [
        ((z * RANKS + r) * feats + y, (y * RANKS + r) * feats + z)
        for z in range(feats)
        for r in range(RANKS)
        for y in range(feats)
    ]
    both = lax.ppermute(both, ("dom", "feat"), pairs)
    slabs = [[z * RANKS + r for r in range(RANKS)] for z in range(feats)]
    got = lax.all_gather(both, "dom", axis=0, tiled=True, axis_index_groups=slabs)
    return got.reshape(RANKS, 2, -1, both.shape[1]).swapaxes(0, 1).reshape(got.shape)


def own_columns(rows, feats):
    columns = [[z * RANKS + r for z in range(feats)] for r in range(RANKS)]
    return lax.all_gather(rows, "dom", axis=0, tiled=False, axis_index_groups=columns)


def swap(blocks, axis, groups=None):
    return lax.all_to_all(blocks, axis, split_axis=0, concat_axis=0, axis_index_groups=groups, tiled=True)


def moved(rows, axis, by):
    size = lax.axis_size(axis)
    return lax.ppermute(rows, axis, [(i, (i + by) % size) for i in range(size)])


def shards(
    first_layer,
    w_first,
    w_second,
    tile_values,
    tile_sources,
    halo_sources,
    send_rows,
    block_counts,
    stale_halo,
):
    count = first_layer.shape[0]
    picks = send_rows[0]
    feats = lax.axis_size("feat")
    sources = tile_sources[0]
    listed = halo_sources[0]
    stale = stale_halo.reshape(listed.shape[0], picks.shape[1], -1)
    near = 2 * RANKS
    groups = picks.shape[0] // near
    far_groups = [[a * near + m for a in range(groups)] for m in range(near)]
    near_groups = [[a * near + m for m in range(near)] for a in range(groups)]
    place = lax.axis_index("feat").astype(i32).reshape(1)
    group = (lax.axis_index("dom") // near).astype(i32).reshape(1)

    leaving, index = pack_first(first_layer, picks, block_counts, groups)
    leaving, index, w_first, w_second, stale = lax.optimization_barrier(
        (leaving, index, w_first, w_second, stale)
    )
    index = [index] + [moved(index, "dom", k * near) for k in range(1, groups)]
    slab = slab_columns(w_first, w_second, feats)
    arrived = swap(leaving, "dom")
    stale_mixed = stale_mixture(first_layer, stale, tile_values, sources)
    rounded = first_mixture(first_layer, arrived, tile_values, sources, listed, feats)
    rounded, slab, stale_mixed, *index = lax.optimization_barrier((rounded, slab, stale_mixed, *index))
    parts = swap(rounded, "feat")
    weights = own_columns(slab, feats)

    hidden = hidden_copies(place, parts, weights, groups)
    spread_hidden = swap(hidden, "dom", far_groups)
    own = second_mixture(hidden, stale_mixed, tile_values, sources)
    before, after = moved(own, "feat", 1), moved(own, "feat", -1)
    spread_hidden, before, after = lax.optimization_barrier((spread_hidden, before, after))
    blocks = pack_second(group, spread_hidden, index, near)
    blocks, before, after = lax.optimization_barrier((blocks, before, after))
    received = swap(blocks, "dom", near_groups).reshape((-1,) + blocks.shape[2:])
    parts = {0: own, 1: before, -1: after}
    parts.update({4: moved(before, "feat", 3), 3: moved(before, "feat", 2), -3: moved(after, "feat", -2)})
    parts.update({2: moved(before, "feat", 1), -2: moved(after, "feat", -1)})
    layer_out = final_rows(place, weights, parts)
    fresh_halo = compact(received, listed, groups)
    return (layer_out, fresh_halo)


def solution(mesh):
    placed = (
        P("dom", "feat"),
        P("feat", "dom"),
        P("feat", "dom"),
        P("dom", None, None, None),
        P("dom", None, None),
        P("dom", None),
        P("dom", None, None),
        P("dom", None),
        P("dom", "feat"),
    )
    return jax.shard_map(
        shards,
        mesh=mesh,
        in_specs=placed,
        out_specs=(P("dom", "feat"), P("dom", "feat")),
        check_vma=False,
    )
```

```python
import math

import jax
import jax.numpy as jnp
from jax import lax
from jax.experimental import pallas as pl
from jax.experimental.pallas import tpu as pltpu
from jax.sharding import PartitionSpec as P

alpha_mix = 0.1
beta_first = math.log(1.5)
beta_second = math.log(1.25)
VMEM_BYTES = 16 * 1024 * 1024
RANKS = 8
SEND = 8
GROUP = 2
bf16 = jnp.bfloat16
f32 = jnp.float32
i32 = jnp.int32
vmem = pl.BlockSpec(memory_space=pltpu.VMEM)
smem = pl.BlockSpec(memory_space=pltpu.SMEM)


def params(limit=VMEM_BYTES):
    return pltpu.CompilerParams(vmem_limit_bytes=limit)


def cost(flops, moved):
    return pl.CostEstimate(flops=flops, bytes_accessed=moved, transcendentals=0)


def in_hbm(*arrays):
    return [pltpu.with_memory_space_constraint(array, pltpu.HBM) for array in arrays]


def dot_nt(left, right):
    return lax.dot_general(left, right, (((1,), (1,)), ((), ())), preferred_element_type=f32)


def fold_rows(rows):
    half = rows.shape[0] // 2
    return jnp.concatenate([rows[:half], rows[half:]], axis=1)


def place_of(picks, counts, half):
    targets = picks.shape[0]
    square = (targets, targets)
    same = lax.broadcasted_iota(i32, square, 0) == lax.broadcasted_iota(i32, square, 1)
    listed = jnp.where(same, jnp.broadcast_to(counts, square), 0)
    listed = jnp.sum(listed, axis=1, keepdims=True)
    high = picks >= half
    live = jnp.logical_and(listed > 0, picks < 2 * half)
    low = jnp.where(live, picks - jnp.where(high, half, 0), half + 44)
    return low.astype(f32), jnp.where(high, 1.0, 0.0)


def turned(rows):
    return jnp.concatenate([rows] * (rows.shape[1] // rows.shape[0]), axis=0).T


def picker(half, slots, width):
    lanes = slots
    places = [
        (lax.broadcasted_iota(i32, (slots, lanes), 1) + first).astype(f32).astype(bf16)
        for first in range(0, half, lanes)
    ]
    one, zero = jnp.ones((slots, lanes), bf16), jnp.zeros((slots, lanes), bf16)

    def pick(folded, low, high):
        wanted = jnp.broadcast_to(low, (slots, lanes)).astype(bf16)
        hot = jnp.concatenate([jnp.where(wanted == place, one, zero) for place in places], axis=1)
        both = jnp.dot(hot, folded, preferred_element_type=f32)
        side = jnp.broadcast_to(high, (slots, width))
        return jnp.where(side > 0.5, both[:, width:], both[:, :width]).astype(bf16)

    return pick


def pack_first_kernel(rows_ref, picks_ref, counts_ref, out_ref, index_ref, blocks_ref, places_ref, sems):
    targets, slots, width = blocks_ref.shape
    groups = index_ref.shape[0]
    half = rows_ref.shape[0] // 2
    low, high = place_of(picks_ref[...], counts_ref[...], half)
    per = targets // groups
    for g in range(groups):
        places_ref[g, 0:per, :] = low[g * per : (g + 1) * per].astype(bf16)
        places_ref[g, per : 2 * per, :] = high[g * per : (g + 1) * per].astype(bf16)
    copies = [pltpu.make_async_copy(places_ref, index_ref, sems.at[targets // SEND])]
    copies[0].start()
    low, high = turned(low), turned(high)
    folded = fold_rows(rows_ref[...])
    pick = picker(half, slots, width)
    for t in range(targets):
        blocks_ref[t] = pick(folded, low[:, t : t + 1], high[:, t : t + 1])
        if (t + 1) % SEND == 0:
            span = pl.ds(t + 1 - SEND, SEND)
            copies.append(pltpu.make_async_copy(blocks_ref.at[span], out_ref.at[span], sems.at[t // SEND]))
            copies[-1].start()
    for copy in copies:
        copy.wait()


def pack_first(rows, picks, counts, groups):
    targets, slots = picks.shape
    count, width = rows.shape
    index = (groups, 2 * targets // groups, slots)
    return pl.pallas_call(
        pack_first_kernel,
        in_specs=[vmem] * 3,
        out_specs=[pl.BlockSpec(memory_space=pltpu.HBM)] * 2,
        out_shape=[pltpu.HBM((targets, slots, width), bf16), pltpu.HBM(index, bf16)],
        scratch_shapes=[
            pltpu.VMEM((targets, slots, width), bf16),
            pltpu.VMEM(index, bf16),
            pltpu.SemaphoreType.DMA((targets // SEND + 1,)),
        ],
        compiler_params=params(),
        cost_estimate=cost(2 * targets * slots * count * width, 3 * 1024 * 1024),
        name="pack_first",
    )(*in_hbm(rows, picks, counts))


def pack_second_kernel(group_ref, rows_ref, *refs):
    groups = rows_ref.shape[0]
    index_refs, (out_ref, blocks_ref, sems) = refs[:groups], refs[groups:]
    targets, _, slots, width = blocks_ref.shape
    half = rows_ref.shape[1] // 2
    own = group_ref[0]
    places = [ref[...].astype(f32) for ref in index_refs]
    low = turned(jnp.concatenate([place[:targets] for place in places], axis=0))
    high = turned(jnp.concatenate([place[targets:] for place in places], axis=0))
    sources = [lax.rem(own + groups - k, groups) for k in range(groups)]
    folded = [fold_rows(rows_ref[source]) for source in sources]
    pick = picker(half, slots, width)
    copies = []
    for t in range(targets):
        for k in range(groups):
            c = k * targets + t
            blocks_ref[t, sources[k]] = pick(folded[k], low[:, c : c + 1], high[:, c : c + 1])
        if (t + 1) % GROUP == 0:
            span = pl.ds(t + 1 - GROUP, GROUP)
            copies.append(pltpu.make_async_copy(blocks_ref.at[span], out_ref.at[span], sems.at[t // GROUP]))
            copies[-1].start()
    for copy in copies:
        copy.wait()


def pack_second(group, rows, index, targets):
    groups, count, width = rows.shape
    shape = (targets, groups, width, width)
    return pl.pallas_call(
        pack_second_kernel,
        in_specs=[smem] + [vmem] * (1 + groups),
        out_specs=pl.BlockSpec(memory_space=pltpu.HBM),
        out_shape=pltpu.HBM(shape, bf16),
        scratch_shapes=[pltpu.VMEM(shape, bf16), pltpu.SemaphoreType.DMA((shape[0] // GROUP,))],
        compiler_params=params(),
        cost_estimate=cost(2 * shape[0] * groups * width * count * width, 3 * 1024 * 1024),
        name="pack_second",
    )(group, rows, *index)


def arrival(source, ranks, groups):
    return lax.rem(source, ranks) * groups + lax.div(source, ranks)


def tile_pairs(tiles_ref, i, firsts, block):
    total = None
    for k in firsts:
        left = jnp.concatenate([tiles_ref[i, k], tiles_ref[i, k + 1]], axis=1)
        right = jnp.concatenate([block(i, k), block(i, k + 1)], axis=0)
        term = jnp.dot(left, right, preferred_element_type=f32)
        total = term if total is None else total + term
    return total


def local_sum(tiles_ref, sources_ref, local_ref, i):
    size = tiles_ref.shape[2]

    def block(i, k):
        return local_ref[pl.ds(pl.multiple_of(sources_ref[i, k] * size, size), size), :]

    return tile_pairs(tiles_ref, i, [0], block)


def halo_sum(tiles_ref, sources_ref, block_of, i):
    blocks, tiles = tiles_ref.shape[0], tiles_ref.shape[1]

    def block(i, k):
        return block_of(sources_ref[i, k] - blocks)

    return tile_pairs(tiles_ref, i, range(2, tiles, 2), block)


def first_kernel(local_ref, halo_ref, tiles_ref, sources_ref, peers_ref, out_ref, rounded_ref, sems):
    size = tiles_ref.shape[2]
    blocks = tiles_ref.shape[0]
    copies = []
    for i in range(blocks):
        total = local_sum(tiles_ref, sources_ref, local_ref, i)
        total = total + halo_sum(tiles_ref, sources_ref, lambda j: halo_ref[peers_ref[j]], i)
        rows = pl.ds(i * size, size)
        mixed = (1.0 - alpha_mix) * total + alpha_mix * local_ref[rows, :].astype(f32)
        rounded_ref[rows, :] = mixed.astype(bf16)
        if i % 2 == 1:
            ready = pl.ds((i - 1) * size, 2 * size)
            for g in range(out_ref.shape[0]):
                copy = pltpu.make_async_copy(rounded_ref.at[ready], out_ref.at[g, ready], sems.at[i // 2, g])
                copy.start()
                copies.append(copy)
    for copy in copies:
        copy.wait()


def first_mixture(rows, halo, tiles, sources, peers, copies):
    count, width = rows.shape
    return pl.pallas_call(
        first_kernel,
        in_specs=[vmem] * 3 + [smem] * 2,
        out_specs=pl.BlockSpec(memory_space=pltpu.HBM),
        out_shape=pltpu.HBM((copies, count, width), bf16),
        scratch_shapes=[pltpu.VMEM((count, width), bf16), pltpu.SemaphoreType.DMA((tiles.shape[0] // 2, copies))],
        compiler_params=params(),
        cost_estimate=cost(170 * 1000 * 1000, 5 * 1024 * 1024),
        name="first_mixture",
    )(rows, halo, tiles, sources, peers)


def stale_kernel(first_ref, stale_ref, tiles_ref, sources_ref, out_ref):
    size = tiles_ref.shape[2]
    for i in range(tiles_ref.shape[0]):
        total = halo_sum(tiles_ref, sources_ref, lambda j: stale_ref[j], i)
        rows = pl.ds(i * size, size)
        out_ref[rows, :] = (1.0 - alpha_mix) * total + alpha_mix * first_ref[rows, :].astype(f32)


def stale_mixture(first_rows, stale, tiles, sources):
    return pl.pallas_call(
        stale_kernel,
        in_specs=[vmem] * 3 + [smem],
        out_specs=vmem,
        out_shape=pltpu.HBM(first_rows.shape, f32),
        compiler_params=params(),
        cost_estimate=cost(140 * 1000 * 1000, 4 * 1024 * 1024),
        name="stale_mixture",
    )(first_rows, stale, tiles, sources)


def second_kernel(hidden_ref, stale_ref, tiles_ref, sources_ref, rounded_ref):
    size = tiles_ref.shape[2]
    for i in range(tiles_ref.shape[0]):
        rows = pl.ds(i * size, size)
        total = local_sum(tiles_ref, sources_ref, hidden_ref.at[0], i)
        rounded_ref[rows, :] = ((1.0 - alpha_mix) * total + stale_ref[rows, :]).astype(bf16)


def second_mixture(hidden_copies, stale_mixed, tiles, sources):
    shape = stale_mixed.shape
    return pl.pallas_call(
        second_kernel,
        grid=(1,),
        in_specs=[
            pl.BlockSpec((1,) + shape, lambda g: (0, 0, 0)),
            pl.BlockSpec(shape, lambda g: (0, 0)),
            pl.BlockSpec((tiles.shape[0], 2) + tiles.shape[2:], lambda g: (0, 0, 0, 0)),
            smem,
        ],
        out_specs=pl.BlockSpec(shape, lambda g: (0, 0)),
        out_shape=jax.ShapeDtypeStruct(shape, bf16),
        compiler_params=params(),
        cost_estimate=cost(34 * 1000 * 1000, 2 * 1024 * 1024),
        name="second_mixture",
    )(*in_hbm(hidden_copies, stale_mixed, tiles), sources)


def columns_of(weight_ref, layer):
    half = weight_ref.shape[1] // 2
    return lambda z: weight_ref[z, pl.ds(layer * half, half), :]


def finished(beta, parts, own, weight_of):
    turned = None
    for (z, first), (zz, second) in zip(parts[::2], parts[1::2]):
        left = jnp.concatenate([first, second], axis=1)
        right = jnp.concatenate([weight_of(z), weight_of(zz)], axis=1)
        term = dot_nt(left, right)
        turned = term if turned is None else turned + term
    return jax.nn.relu((1.0 - beta) * own.astype(f32) + beta * turned).astype(bf16)


def hidden_kernel(place_ref, parts_ref, weight_ref, out_ref, hidden_ref, sems):
    parts = [(z, parts_ref[z]) for z in range(parts_ref.shape[0])]
    hidden_ref[...] = finished(beta_first, parts, parts_ref[place_ref[0]], columns_of(weight_ref, 0))
    copies = [
        pltpu.make_async_copy(hidden_ref, out_ref.at[g], sems.at[g]) for g in range(out_ref.shape[0])
    ]
    for copy in copies:
        copy.start()
    for copy in copies:
        copy.wait()


def hidden_copies(place, parts, weights, groups):
    shape = parts.shape[1:]
    return pl.pallas_call(
        hidden_kernel,
        in_specs=[smem] + [vmem] * 2,
        out_specs=pl.BlockSpec(memory_space=pltpu.HBM),
        out_shape=pltpu.HBM((groups,) + shape, bf16),
        scratch_shapes=[pltpu.VMEM(shape, bf16), pltpu.SemaphoreType.DMA((groups,))],
        compiler_params=params(),
        cost_estimate=cost(134 * 1000 * 1000, 3 * 1024 * 1024),
        name="hidden",
    )(place, parts, weights)


def final_kernel(places, place_ref, weight_ref, *refs):
    feats = len(places)
    parts = [(lax.rem(place_ref[0] + (feats - k), feats), ref[...]) for k, ref in zip(places, refs)]
    refs[-1][...] = finished(beta_second, parts, refs[0][...], columns_of(weight_ref, 1))


def final_rows(place, weights, parts):
    places = list(parts)

    def kernel(*refs):
        final_kernel(places, *refs)

    return pl.pallas_call(
        kernel,
        in_specs=[smem] + [vmem] * (1 + len(parts)),
        out_specs=vmem,
        out_shape=jax.ShapeDtypeStruct(parts[0].shape, bf16),
        compiler_params=params(),
        cost_estimate=cost(134 * 1000 * 1000, 3 * 1024 * 1024),
        name="final_rows",
    )(place, weights, *parts.values())


def compact_kernel(groups, peers_ref, arrived_ref, out_ref, sems):
    ranks = arrived_ref.shape[0] // groups
    copies = [
        pltpu.make_async_copy(
            arrived_ref.at[arrival(peers_ref[j], ranks, groups)], out_ref.at[j], sems.at[j]
        )
        for j in range(out_ref.shape[0])
    ]
    for copy in copies:
        copy.start()
    for copy in copies:
        copy.wait()


def compact(arrived, peers, groups):
    shape = (peers.shape[0],) + arrived.shape[1:]

    def kernel(*refs):
        compact_kernel(groups, *refs)

    out = pl.pallas_call(
        kernel,
        in_specs=[smem, vmem],
        out_specs=pl.BlockSpec(memory_space=pl.ANY),
        out_shape=jax.ShapeDtypeStruct(shape, arrived.dtype),
        scratch_shapes=[pltpu.SemaphoreType.DMA((shape[0],))],
        compiler_params=params(),
        cost_estimate=cost(0, 2 * 1024 * 1024),
        name="compact",
    )(peers, arrived)
    return out.reshape(-1, arrived.shape[2])


def slab_columns(w_first, w_second, feats):
    both = jnp.concatenate([w_first.T, w_second.T], axis=0)
    pairs = [
        ((z * RANKS + r) * feats + y, (y * RANKS + r) * feats + z)
        for z in range(feats)
        for r in range(RANKS)
        for y in range(feats)
    ]
    both = lax.ppermute(both, ("dom", "feat"), pairs)
    slabs = [[z * RANKS + r for r in range(RANKS)] for z in range(feats)]
    got = lax.all_gather(both, "dom", axis=0, tiled=True, axis_index_groups=slabs)
    return got.reshape(RANKS, 2, -1, both.shape[1]).swapaxes(0, 1).reshape(got.shape)


def own_columns(rows, feats):
    columns = [[z * RANKS + r for z in range(feats)] for r in range(RANKS)]
    return lax.all_gather(rows, "dom", axis=0, tiled=False, axis_index_groups=columns)


def swap(blocks, axis, groups=None):
    return lax.all_to_all(blocks, axis, split_axis=0, concat_axis=0, axis_index_groups=groups, tiled=True)


def moved(rows, axis, by):
    size = lax.axis_size(axis)
    return lax.ppermute(rows, axis, [(i, (i + by) % size) for i in range(size)])


def shards(
    first_layer,
    w_first,
    w_second,
    tile_values,
    tile_sources,
    halo_sources,
    send_rows,
    block_counts,
    stale_halo,
):
    count = first_layer.shape[0]
    picks = send_rows[0]
    feats = lax.axis_size("feat")
    sources = tile_sources[0]
    listed = halo_sources[0]
    stale = stale_halo.reshape(listed.shape[0], picks.shape[1], -1)
    near = 2 * RANKS
    groups = picks.shape[0] // near
    far_groups = [[a * near + m for a in range(groups)] for m in range(near)]
    near_groups = [[a * near + m for m in range(near)] for a in range(groups)]
    place = lax.axis_index("feat").astype(i32).reshape(1)
    group = (lax.axis_index("dom") // near).astype(i32).reshape(1)

    leaving, index = pack_first(first_layer, picks, block_counts, groups)
    leaving, index, w_first, w_second, stale = lax.optimization_barrier(
        (leaving, index, w_first, w_second, stale)
    )
    index = [
        lax.dynamic_index_in_dim(index, lax.rem(group[0] + k, groups), keepdims=False) for k in range(groups)
    ]
    index = index[:1] + [moved(index[k], "dom", k * near) for k in range(1, groups)]
    slab = slab_columns(w_first, w_second, feats)
    arrived = swap(leaving, "dom")
    stale_mixed = stale_mixture(first_layer, stale, tile_values, sources)
    rounded = first_mixture(first_layer, arrived, tile_values, sources, listed, feats)
    rounded, slab, stale_mixed, *index = lax.optimization_barrier((rounded, slab, stale_mixed, *index))
    parts = swap(rounded, "feat")
    weights = own_columns(slab, feats)

    hidden = hidden_copies(place, parts, weights, groups)
    spread_hidden = swap(hidden, "dom", far_groups)
    own = second_mixture(hidden, stale_mixed, tile_values, sources)
    before, after = moved(own, "feat", 1), moved(own, "feat", -1)
    blocks = pack_second(group, spread_hidden, index, near)
    blocks, before, after = lax.optimization_barrier((blocks, before, after))
    received = swap(blocks, "dom", near_groups).reshape((-1,) + blocks.shape[2:])
    parts = {0: own, 1: before, -1: after}
    parts.update({4: moved(before, "feat", 3), 3: moved(before, "feat", 2), -3: moved(after, "feat", -2)})
    parts.update({2: moved(before, "feat", 1), -2: moved(after, "feat", -1)})
    layer_out = final_rows(place, weights, parts)
    fresh_halo = compact(received, listed, groups)
    return (layer_out, fresh_halo)


def solution(mesh):
    placed = (
        P("dom", "feat"),
        P("feat", "dom"),
        P("feat", "dom"),
        P("dom", None, None, None),
        P("dom", None, None),
        P("dom", None),
        P("dom", None, None),
        P("dom", None),
        P("dom", "feat"),
    )
    return jax.shard_map(
        shards,
        mesh=mesh,
        in_specs=placed,
        out_specs=(P("dom", "feat"), P("dom", "feat")),
        check_vma=False,
    )
```

```python
import math

import jax
import jax.numpy as jnp
from jax import lax
from jax.experimental import pallas as pl
from jax.experimental.pallas import tpu as pltpu
from jax.sharding import PartitionSpec as P

alpha_mix = 0.1
beta_first = math.log(1.5)
beta_second = math.log(1.25)
VMEM_BYTES = 16 * 1024 * 1024
RANKS = 8
SEND = 8
GROUP = 2
bf16 = jnp.bfloat16
f32 = jnp.float32
i32 = jnp.int32
vmem = pl.BlockSpec(memory_space=pltpu.VMEM)
smem = pl.BlockSpec(memory_space=pltpu.SMEM)


def params(limit=VMEM_BYTES):
    return pltpu.CompilerParams(vmem_limit_bytes=limit)


def cost(flops, moved):
    return pl.CostEstimate(flops=flops, bytes_accessed=moved, transcendentals=0)


def in_hbm(*arrays):
    return [pltpu.with_memory_space_constraint(array, pltpu.HBM) for array in arrays]


def dot_nt(left, right):
    return lax.dot_general(left, right, (((1,), (1,)), ((), ())), preferred_element_type=f32)


def fold_rows(rows):
    half = rows.shape[0] // 2
    return jnp.concatenate([rows[:half], rows[half:]], axis=1)


def place_of(picks, counts, half):
    targets = picks.shape[0]
    square = (targets, targets)
    same = lax.broadcasted_iota(i32, square, 0) == lax.broadcasted_iota(i32, square, 1)
    listed = jnp.where(same, jnp.broadcast_to(counts, square), 0)
    listed = jnp.sum(listed, axis=1, keepdims=True)
    high = picks >= half
    live = jnp.logical_and(listed > 0, picks < 2 * half)
    low = jnp.where(live, picks - jnp.where(high, half, 0), half + 44)
    return low.astype(f32), jnp.where(high, 1.0, 0.0)


def turned(rows):
    return jnp.concatenate([rows] * (rows.shape[1] // rows.shape[0]), axis=0).T


def picker(half, slots, width):
    lanes = slots
    places = [
        (lax.broadcasted_iota(i32, (slots, lanes), 1) + first).astype(f32).astype(bf16)
        for first in range(0, half, lanes)
    ]
    one, zero = jnp.ones((slots, lanes), bf16), jnp.zeros((slots, lanes), bf16)

    def pick(folded, low, high):
        wanted = jnp.broadcast_to(low, (slots, lanes)).astype(bf16)
        hot = jnp.concatenate([jnp.where(wanted == place, one, zero) for place in places], axis=1)
        both = jnp.dot(hot, folded, preferred_element_type=f32)
        side = jnp.broadcast_to(high, (slots, width))
        return jnp.where(side > 0.5, both[:, width:], both[:, :width]).astype(bf16)

    return pick


def pack_first_kernel(rows_ref, picks_ref, counts_ref, out_ref, index_ref, blocks_ref, places_ref, sems):
    targets, slots, width = blocks_ref.shape
    groups = index_ref.shape[0]
    half = rows_ref.shape[0] // 2
    low, high = place_of(picks_ref[...], counts_ref[...], half)
    per = targets // groups
    for g in range(groups):
        places_ref[g, 0:per, :] = low[g * per : (g + 1) * per].astype(bf16)
        places_ref[g, per : 2 * per, :] = high[g * per : (g + 1) * per].astype(bf16)
    copies = [pltpu.make_async_copy(places_ref, index_ref, sems.at[targets // SEND])]
    copies[0].start()
    low, high = turned(low), turned(high)
    folded = fold_rows(rows_ref[...])
    pick = picker(half, slots, width)
    for t in range(targets):
        blocks_ref[t] = pick(folded, low[:, t : t + 1], high[:, t : t + 1])
        if (t + 1) % SEND == 0:
            span = pl.ds(t + 1 - SEND, SEND)
            copies.append(pltpu.make_async_copy(blocks_ref.at[span], out_ref.at[span], sems.at[t // SEND]))
            copies[-1].start()
    for copy in copies:
        copy.wait()


def pack_first(rows, picks, counts, groups):
    targets, slots = picks.shape
    count, width = rows.shape
    index = (groups, 2 * targets // groups, slots)
    return pl.pallas_call(
        pack_first_kernel,
        in_specs=[vmem] * 3,
        out_specs=[pl.BlockSpec(memory_space=pltpu.HBM)] * 2,
        out_shape=[pltpu.HBM((targets, slots, width), bf16), pltpu.HBM(index, bf16)],
        scratch_shapes=[
            pltpu.VMEM((targets, slots, width), bf16),
            pltpu.VMEM(index, bf16),
            pltpu.SemaphoreType.DMA((targets // SEND + 1,)),
        ],
        compiler_params=params(),
        cost_estimate=cost(2 * targets * slots * count * width, 3 * 1024 * 1024),
        name="pack_first",
    )(*in_hbm(rows, picks, counts))


def pack_second_kernel(rows_ref, columns_ref, out_ref, blocks_ref, sems):
    targets, groups, slots, width = blocks_ref.shape
    low, high = columns_ref[0].astype(f32), columns_ref[1].astype(f32)
    folded = [fold_rows(rows_ref[a]) for a in range(groups)]
    pick = picker(rows_ref.shape[1] // 2, slots, width)
    copies = []
    for t in range(targets):
        for a in range(groups):
            c = a * targets + t
            blocks_ref[t, a] = pick(folded[a], low[:, c : c + 1], high[:, c : c + 1])
        if (t + 1) % GROUP == 0:
            span = pl.ds(t + 1 - GROUP, GROUP)
            copies.append(pltpu.make_async_copy(blocks_ref.at[span], out_ref.at[span], sems.at[t // GROUP]))
            copies[-1].start()
    for copy in copies:
        copy.wait()


def pack_second(rows, columns, targets):
    groups, count, width = rows.shape
    shape = (targets, groups, width, width)
    return pl.pallas_call(
        pack_second_kernel,
        in_specs=[vmem] * 2,
        out_specs=pl.BlockSpec(memory_space=pltpu.HBM),
        out_shape=pltpu.HBM(shape, bf16),
        scratch_shapes=[pltpu.VMEM(shape, bf16), pltpu.SemaphoreType.DMA((shape[0] // GROUP,))],
        compiler_params=params(),
        cost_estimate=cost(2 * shape[0] * groups * width * count * width, 3 * 1024 * 1024),
        name="pack_second",
    )(rows, columns)


def arrival(source, ranks, groups):
    return lax.rem(source, ranks) * groups + lax.div(source, ranks)


def tile_pairs(tiles_ref, i, firsts, block):
    total = None
    for k in firsts:
        left = jnp.concatenate([tiles_ref[i, k], tiles_ref[i, k + 1]], axis=1)
        right = jnp.concatenate([block(i, k), block(i, k + 1)], axis=0)
        term = jnp.dot(left, right, preferred_element_type=f32)
        total = term if total is None else total + term
    return total


def local_sum(tiles_ref, sources_ref, local_ref, i):
    size = tiles_ref.shape[2]

    def block(i, k):
        return local_ref[pl.ds(pl.multiple_of(sources_ref[i, k] * size, size), size), :]

    return tile_pairs(tiles_ref, i, [0], block)


def halo_sum(tiles_ref, sources_ref, block_of, i):
    blocks, tiles = tiles_ref.shape[0], tiles_ref.shape[1]

    def block(i, k):
        return block_of(sources_ref[i, k] - blocks)

    return tile_pairs(tiles_ref, i, range(2, tiles, 2), block)


def first_kernel(local_ref, halo_ref, tiles_ref, sources_ref, peers_ref, out_ref, rounded_ref, sems):
    size = tiles_ref.shape[2]
    blocks = tiles_ref.shape[0]
    copies = []
    for i in range(blocks):
        total = local_sum(tiles_ref, sources_ref, local_ref, i)
        total = total + halo_sum(tiles_ref, sources_ref, lambda j: halo_ref[peers_ref[j]], i)
        rows = pl.ds(i * size, size)
        mixed = (1.0 - alpha_mix) * total + alpha_mix * local_ref[rows, :].astype(f32)
        rounded_ref[rows, :] = mixed.astype(bf16)
        if i % 2 == 1:
            ready = pl.ds((i - 1) * size, 2 * size)
            for g in range(out_ref.shape[0]):
                copy = pltpu.make_async_copy(rounded_ref.at[ready], out_ref.at[g, ready], sems.at[i // 2, g])
                copy.start()
                copies.append(copy)
    for copy in copies:
        copy.wait()


def first_mixture(rows, halo, tiles, sources, peers, copies):
    count, width = rows.shape
    return pl.pallas_call(
        first_kernel,
        in_specs=[vmem] * 3 + [smem] * 2,
        out_specs=pl.BlockSpec(memory_space=pltpu.HBM),
        out_shape=pltpu.HBM((copies, count, width), bf16),
        scratch_shapes=[pltpu.VMEM((count, width), bf16), pltpu.SemaphoreType.DMA((tiles.shape[0] // 2, copies))],
        compiler_params=params(),
        cost_estimate=cost(170 * 1000 * 1000, 5 * 1024 * 1024),
        name="first_mixture",
    )(rows, halo, tiles, sources, peers)


def stale_kernel(first_ref, stale_ref, tiles_ref, sources_ref, out_ref):
    size = tiles_ref.shape[2]
    for i in range(tiles_ref.shape[0]):
        total = halo_sum(tiles_ref, sources_ref, lambda j: stale_ref[j], i)
        rows = pl.ds(i * size, size)
        out_ref[rows, :] = (1.0 - alpha_mix) * total + alpha_mix * first_ref[rows, :].astype(f32)


def stale_mixture(first_rows, stale, tiles, sources):
    return pl.pallas_call(
        stale_kernel,
        in_specs=[vmem] * 3 + [smem],
        out_specs=vmem,
        out_shape=pltpu.HBM(first_rows.shape, f32),
        compiler_params=params(),
        cost_estimate=cost(140 * 1000 * 1000, 4 * 1024 * 1024),
        name="stale_mixture",
    )(first_rows, stale, tiles, sources)


def second_kernel(sources_ref, group_ref, hidden_ref, stale_ref, tiles_ref, *refs):
    index_refs, (rounded_ref, columns_ref, low_ref, high_ref) = refs[:-4], refs[-4:]
    groups = len(index_refs)
    targets = index_refs[0].shape[0] // 2
    size = tiles_ref.shape[2]
    for i in range(tiles_ref.shape[0]):
        rows = pl.ds(i * size, size)
        total = local_sum(tiles_ref, sources_ref, hidden_ref.at[0], i)
        rounded_ref[rows, :] = ((1.0 - alpha_mix) * total + stale_ref[rows, :]).astype(bf16)
    for k, ref in enumerate(index_refs):
        source = lax.rem(group_ref[0] + groups - k, groups)
        span = pl.ds(pl.multiple_of(source * targets, targets), targets)
        place = ref[...].astype(f32)
        low_ref[span, :] = place[:targets]
        high_ref[span, :] = place[targets:]
    columns_ref[0] = turned(low_ref[...]).astype(bf16)
    columns_ref[1] = turned(high_ref[...]).astype(bf16)


def second_mixture(group, hidden_copies, stale_mixed, tiles, sources, index):
    shape = stale_mixed.shape
    used = len(index) * index[0].shape[0] // 2
    square = (2, shape[1], shape[1])
    return pl.pallas_call(
        second_kernel,
        grid=(1,),
        in_specs=[smem] * 2
        + [
            pl.BlockSpec((1,) + shape, lambda g: (0, 0, 0)),
            pl.BlockSpec(shape, lambda g: (0, 0)),
            pl.BlockSpec((tiles.shape[0], 2) + tiles.shape[2:], lambda g: (0, 0, 0, 0)),
        ]
        + [pl.BlockSpec(index[0].shape, lambda g: (0, 0))] * len(index),
        out_specs=[pl.BlockSpec(shape, lambda g: (0, 0)), pl.BlockSpec(square, lambda g: (0, 0, 0))],
        out_shape=[jax.ShapeDtypeStruct(shape, bf16), jax.ShapeDtypeStruct(square, bf16)],
        scratch_shapes=[pltpu.VMEM((used, shape[1]), f32)] * 2,
        compiler_params=params(),
        cost_estimate=cost(34 * 1000 * 1000, 2 * 1024 * 1024),
        name="second_mixture",
    )(sources, group, *in_hbm(hidden_copies, stale_mixed, tiles), *index)


def columns_of(weight_ref, layer):
    half = weight_ref.shape[1] // 2
    return lambda z: weight_ref[z, pl.ds(layer * half, half), :]


def finished(beta, parts, own, weight_of):
    turned = None
    for (z, first), (zz, second) in zip(parts[::2], parts[1::2]):
        left = jnp.concatenate([first, second], axis=1)
        right = jnp.concatenate([weight_of(z), weight_of(zz)], axis=1)
        term = dot_nt(left, right)
        turned = term if turned is None else turned + term
    return jax.nn.relu((1.0 - beta) * own.astype(f32) + beta * turned).astype(bf16)


def hidden_kernel(place_ref, parts_ref, weight_ref, out_ref, hidden_ref, sems):
    parts = [(z, parts_ref[z]) for z in range(parts_ref.shape[0])]
    hidden_ref[...] = finished(beta_first, parts, parts_ref[place_ref[0]], columns_of(weight_ref, 0))
    copies = [
        pltpu.make_async_copy(hidden_ref, out_ref.at[g], sems.at[g]) for g in range(out_ref.shape[0])
    ]
    for copy in copies:
        copy.start()
    for copy in copies:
        copy.wait()


def hidden_copies(place, parts, weights, groups):
    shape = parts.shape[1:]
    return pl.pallas_call(
        hidden_kernel,
        in_specs=[smem] + [vmem] * 2,
        out_specs=pl.BlockSpec(memory_space=pltpu.HBM),
        out_shape=pltpu.HBM((groups,) + shape, bf16),
        scratch_shapes=[pltpu.VMEM(shape, bf16), pltpu.SemaphoreType.DMA((groups,))],
        compiler_params=params(),
        cost_estimate=cost(134 * 1000 * 1000, 3 * 1024 * 1024),
        name="hidden",
    )(place, parts, weights)


def final_kernel(places, place_ref, weight_ref, *refs):
    feats = len(places)
    parts = [(lax.rem(place_ref[0] + (feats - k), feats), ref[...]) for k, ref in zip(places, refs)]
    refs[-1][...] = finished(beta_second, parts, refs[0][...], columns_of(weight_ref, 1))


def final_rows(place, weights, parts):
    places = list(parts)

    def kernel(*refs):
        final_kernel(places, *refs)

    return pl.pallas_call(
        kernel,
        in_specs=[smem] + [vmem] * (1 + len(parts)),
        out_specs=vmem,
        out_shape=jax.ShapeDtypeStruct(parts[0].shape, bf16),
        compiler_params=params(),
        cost_estimate=cost(134 * 1000 * 1000, 3 * 1024 * 1024),
        name="final_rows",
    )(place, weights, *parts.values())


def compact_kernel(groups, peers_ref, arrived_ref, out_ref, sems):
    ranks = arrived_ref.shape[0] // groups
    copies = [
        pltpu.make_async_copy(
            arrived_ref.at[arrival(peers_ref[j], ranks, groups)], out_ref.at[j], sems.at[j]
        )
        for j in range(out_ref.shape[0])
    ]
    for copy in copies:
        copy.start()
    for copy in copies:
        copy.wait()


def compact(arrived, peers, groups):
    shape = (peers.shape[0],) + arrived.shape[1:]

    def kernel(*refs):
        compact_kernel(groups, *refs)

    out = pl.pallas_call(
        kernel,
        in_specs=[smem, vmem],
        out_specs=pl.BlockSpec(memory_space=pl.ANY),
        out_shape=jax.ShapeDtypeStruct(shape, arrived.dtype),
        scratch_shapes=[pltpu.SemaphoreType.DMA((shape[0],))],
        compiler_params=params(),
        cost_estimate=cost(0, 2 * 1024 * 1024),
        name="compact",
    )(peers, arrived)
    return out.reshape(-1, arrived.shape[2])


def slab_columns(w_first, w_second, feats):
    both = jnp.concatenate([w_first.T, w_second.T], axis=0)
    pairs = [
        ((z * RANKS + r) * feats + y, (y * RANKS + r) * feats + z)
        for z in range(feats)
        for r in range(RANKS)
        for y in range(feats)
    ]
    both = lax.ppermute(both, ("dom", "feat"), pairs)
    slabs = [[z * RANKS + r for r in range(RANKS)] for z in range(feats)]
    got = lax.all_gather(both, "dom", axis=0, tiled=True, axis_index_groups=slabs)
    return got.reshape(RANKS, 2, -1, both.shape[1]).swapaxes(0, 1).reshape(got.shape)


def own_columns(rows, feats):
    columns = [[z * RANKS + r for z in range(feats)] for r in range(RANKS)]
    return lax.all_gather(rows, "dom", axis=0, tiled=False, axis_index_groups=columns)


def swap(blocks, axis, groups=None):
    return lax.all_to_all(blocks, axis, split_axis=0, concat_axis=0, axis_index_groups=groups, tiled=True)


def moved(rows, axis, by):
    size = lax.axis_size(axis)
    return lax.ppermute(rows, axis, [(i, (i + by) % size) for i in range(size)])


def shards(
    first_layer,
    w_first,
    w_second,
    tile_values,
    tile_sources,
    halo_sources,
    send_rows,
    block_counts,
    stale_halo,
):
    count = first_layer.shape[0]
    picks = send_rows[0]
    feats = lax.axis_size("feat")
    sources = tile_sources[0]
    listed = halo_sources[0]
    stale = stale_halo.reshape(listed.shape[0], picks.shape[1], -1)
    near = 2 * RANKS
    groups = picks.shape[0] // near
    far_groups = [[a * near + m for a in range(groups)] for m in range(near)]
    near_groups = [[a * near + m for m in range(near)] for a in range(groups)]
    place = lax.axis_index("feat").astype(i32).reshape(1)
    group = (lax.axis_index("dom") // near).astype(i32).reshape(1)

    leaving, index = pack_first(first_layer, picks, block_counts, groups)
    leaving, index, w_first, w_second, stale = lax.optimization_barrier(
        (leaving, index, w_first, w_second, stale)
    )
    index = [
        lax.dynamic_index_in_dim(index, lax.rem(group[0] + k, groups), keepdims=False) for k in range(groups)
    ]
    index = index[:1] + [moved(index[k], "dom", k * near) for k in range(1, groups)]
    slab = slab_columns(w_first, w_second, feats)
    arrived = swap(leaving, "dom")
    stale_mixed = stale_mixture(first_layer, stale, tile_values, sources)
    rounded = first_mixture(first_layer, arrived, tile_values, sources, listed, feats)
    rounded, slab, stale_mixed, *index = lax.optimization_barrier((rounded, slab, stale_mixed, *index))
    parts = swap(rounded, "feat")
    weights = own_columns(slab, feats)

    hidden = hidden_copies(place, parts, weights, groups)
    spread_hidden = swap(hidden, "dom", far_groups)
    own, columns = second_mixture(group, hidden, stale_mixed, tile_values, sources, index)
    before, after = moved(own, "feat", 1), moved(own, "feat", -1)
    blocks = pack_second(spread_hidden, columns, near)
    blocks, before, after = lax.optimization_barrier((blocks, before, after))
    received = swap(blocks, "dom", near_groups).reshape((-1,) + blocks.shape[2:])
    parts = {0: own, 1: before, -1: after}
    parts.update({4: moved(before, "feat", 3), 3: moved(before, "feat", 2), -3: moved(after, "feat", -2)})
    parts.update({2: moved(before, "feat", 1), -2: moved(after, "feat", -1)})
    layer_out = final_rows(place, weights, parts)
    fresh_halo = compact(received, listed, groups)
    return (layer_out, fresh_halo)


def solution(mesh):
    placed = (
        P("dom", "feat"),
        P("feat", "dom"),
        P("feat", "dom"),
        P("dom", None, None, None),
        P("dom", None, None),
        P("dom", None),
        P("dom", None, None),
        P("dom", None),
        P("dom", "feat"),
    )
    return jax.shard_map(
        shards,
        mesh=mesh,
        in_specs=placed,
        out_specs=(P("dom", "feat"), P("dom", "feat")),
        check_vma=False,
    )
```

```python
import math

import jax
import jax.numpy as jnp
from jax import lax
from jax.experimental import pallas as pl
from jax.experimental.pallas import tpu as pltpu
from jax.sharding import PartitionSpec as P

alpha_mix = 0.1
beta_first = math.log(1.5)
beta_second = math.log(1.25)
VMEM_BYTES = 16 * 1024 * 1024
RANKS = 8
SEND = 8
GROUP = 2
bf16 = jnp.bfloat16
f32 = jnp.float32
i32 = jnp.int32
vmem = pl.BlockSpec(memory_space=pltpu.VMEM)
smem = pl.BlockSpec(memory_space=pltpu.SMEM)


def params(limit=VMEM_BYTES):
    return pltpu.CompilerParams(vmem_limit_bytes=limit)


def cost(flops, moved):
    return pl.CostEstimate(flops=flops, bytes_accessed=moved, transcendentals=0)


def in_hbm(*arrays):
    return [pltpu.with_memory_space_constraint(array, pltpu.HBM) for array in arrays]


def dot_nt(left, right):
    return lax.dot_general(left, right, (((1,), (1,)), ((), ())), preferred_element_type=f32)


def fold_rows(rows):
    half = rows.shape[0] // 2
    return jnp.concatenate([rows[:half], rows[half:]], axis=1)


def place_of(picks, counts, half):
    targets = picks.shape[0]
    square = (targets, targets)
    same = lax.broadcasted_iota(i32, square, 0) == lax.broadcasted_iota(i32, square, 1)
    listed = jnp.where(same, jnp.broadcast_to(counts, square), 0)
    listed = jnp.sum(listed, axis=1, keepdims=True)
    high = picks >= half
    live = jnp.logical_and(listed > 0, picks < 2 * half)
    low = jnp.where(live, picks - jnp.where(high, half, 0), half + 44)
    return low.astype(f32), jnp.where(high, 1.0, 0.0)


def turned(rows):
    return jnp.concatenate([rows] * (rows.shape[1] // rows.shape[0]), axis=0).T


def picker(half, slots, width):
    lanes = slots
    places = [
        (lax.broadcasted_iota(i32, (slots, lanes), 1) + first).astype(f32).astype(bf16)
        for first in range(0, half, lanes)
    ]
    one, zero = jnp.ones((slots, lanes), bf16), jnp.zeros((slots, lanes), bf16)

    def pick(folded, low, high):
        wanted = jnp.broadcast_to(low, (slots, lanes)).astype(bf16)
        hot = jnp.concatenate([jnp.where(wanted == place, one, zero) for place in places], axis=1)
        both = jnp.dot(hot, folded, preferred_element_type=f32)
        side = jnp.broadcast_to(high, (slots, width))
        return jnp.where(side > 0.5, both[:, width:], both[:, :width]).astype(bf16)

    return pick


def pack_first_kernel(rows_ref, picks_ref, counts_ref, out_ref, index_ref, blocks_ref, places_ref, sems):
    targets, slots, width = blocks_ref.shape
    groups = index_ref.shape[0]
    half = rows_ref.shape[0] // 2
    low, high = place_of(picks_ref[...], counts_ref[...], half)
    per = targets // groups
    for g in range(groups):
        places_ref[g, 0:per, :] = low[g * per : (g + 1) * per].astype(bf16)
        places_ref[g, per : 2 * per, :] = high[g * per : (g + 1) * per].astype(bf16)
    copies = [pltpu.make_async_copy(places_ref, index_ref, sems.at[targets // SEND])]
    copies[0].start()
    low, high = turned(low), turned(high)
    folded = fold_rows(rows_ref[...])
    pick = picker(half, slots, width)
    for t in range(targets):
        blocks_ref[t] = pick(folded, low[:, t : t + 1], high[:, t : t + 1])
        if (t + 1) % SEND == 0:
            span = pl.ds(t + 1 - SEND, SEND)
            copies.append(pltpu.make_async_copy(blocks_ref.at[span], out_ref.at[span], sems.at[t // SEND]))
            copies[-1].start()
    for copy in copies:
        copy.wait()


def pack_first(rows, picks, counts, groups):
    targets, slots = picks.shape
    count, width = rows.shape
    index = (groups, 2 * targets // groups, slots)
    return pl.pallas_call(
        pack_first_kernel,
        in_specs=[vmem] * 3,
        out_specs=[pl.BlockSpec(memory_space=pltpu.HBM)] * 2,
        out_shape=[pltpu.HBM((targets, slots, width), bf16), pltpu.HBM(index, bf16)],
        scratch_shapes=[
            pltpu.VMEM((targets, slots, width), bf16),
            pltpu.VMEM(index, bf16),
            pltpu.SemaphoreType.DMA((targets // SEND + 1,)),
        ],
        compiler_params=params(),
        cost_estimate=cost(2 * targets * slots * count * width, 3 * 1024 * 1024),
        name="pack_first",
    )(*in_hbm(rows, picks, counts))


def pack_second_kernel(rows_ref, columns_ref, out_ref, blocks_ref, sems):
    targets, groups, slots, width = blocks_ref.shape
    low, high = columns_ref[0].astype(f32), columns_ref[1].astype(f32)
    folded = [fold_rows(rows_ref[a]) for a in range(groups)]
    pick = picker(rows_ref.shape[1] // 2, slots, width)
    copies = []
    for t in range(targets):
        for a in range(groups):
            c = a * targets + t
            blocks_ref[t, a] = pick(folded[a], low[:, c : c + 1], high[:, c : c + 1])
        if (t + 1) % GROUP == 0:
            span = pl.ds(t + 1 - GROUP, GROUP)
            copies.append(pltpu.make_async_copy(blocks_ref.at[span], out_ref.at[span], sems.at[t // GROUP]))
            copies[-1].start()
    for copy in copies:
        copy.wait()


def pack_second(rows, columns, targets):
    groups, count, width = rows.shape
    shape = (targets, groups, width, width)
    return pl.pallas_call(
        pack_second_kernel,
        in_specs=[vmem] * 2,
        out_specs=pl.BlockSpec(memory_space=pltpu.HBM),
        out_shape=pltpu.HBM(shape, bf16),
        scratch_shapes=[pltpu.VMEM(shape, bf16), pltpu.SemaphoreType.DMA((shape[0] // GROUP,))],
        compiler_params=params(),
        cost_estimate=cost(2 * shape[0] * groups * width * count * width, 3 * 1024 * 1024),
        name="pack_second",
    )(rows, columns)


def arrival(source, ranks, groups):
    return lax.rem(source, ranks) * groups + lax.div(source, ranks)


def tile_pairs(tiles_ref, i, firsts, block):
    total = None
    for k in firsts:
        left = jnp.concatenate([tiles_ref[i, k], tiles_ref[i, k + 1]], axis=1)
        right = jnp.concatenate([block(i, k), block(i, k + 1)], axis=0)
        term = jnp.dot(left, right, preferred_element_type=f32)
        total = term if total is None else total + term
    return total


def local_sum(tiles_ref, sources_ref, local_ref, i):
    size = tiles_ref.shape[2]

    def block(i, k):
        return local_ref[pl.ds(pl.multiple_of(sources_ref[i, k] * size, size), size), :]

    return tile_pairs(tiles_ref, i, [0], block)


def halo_sum(tiles_ref, sources_ref, block_of, i):
    blocks, tiles = tiles_ref.shape[0], tiles_ref.shape[1]

    def block(i, k):
        return block_of(sources_ref[i, k] - blocks)

    return tile_pairs(tiles_ref, i, range(2, tiles, 2), block)


def first_kernel(local_ref, halo_ref, tiles_ref, sources_ref, peers_ref, out_ref, rounded_ref, sems):
    size = tiles_ref.shape[2]
    blocks = tiles_ref.shape[0]
    copies = []
    for i in range(blocks):
        total = local_sum(tiles_ref, sources_ref, local_ref, i)
        total = total + halo_sum(tiles_ref, sources_ref, lambda j: halo_ref[peers_ref[j]], i)
        rows = pl.ds(i * size, size)
        mixed = (1.0 - alpha_mix) * total + alpha_mix * local_ref[rows, :].astype(f32)
        rounded_ref[rows, :] = mixed.astype(bf16)
        if i % 2 == 1:
            ready = pl.ds((i - 1) * size, 2 * size)
            for g in range(out_ref.shape[0]):
                copy = pltpu.make_async_copy(rounded_ref.at[ready], out_ref.at[g, ready], sems.at[i // 2, g])
                copy.start()
                copies.append(copy)
    for copy in copies:
        copy.wait()


def first_mixture(rows, halo, tiles, sources, peers, copies):
    count, width = rows.shape
    return pl.pallas_call(
        first_kernel,
        in_specs=[vmem] * 3 + [smem] * 2,
        out_specs=pl.BlockSpec(memory_space=pltpu.HBM),
        out_shape=pltpu.HBM((copies, count, width), bf16),
        scratch_shapes=[pltpu.VMEM((count, width), bf16), pltpu.SemaphoreType.DMA((tiles.shape[0] // 2, copies))],
        compiler_params=params(),
        cost_estimate=cost(170 * 1000 * 1000, 5 * 1024 * 1024),
        name="first_mixture",
    )(rows, halo, tiles, sources, peers)


def stale_kernel(first_ref, stale_ref, tiles_ref, sources_ref, out_ref):
    size = tiles_ref.shape[2]
    for i in range(tiles_ref.shape[0]):
        total = halo_sum(tiles_ref, sources_ref, lambda j: stale_ref[j], i)
        rows = pl.ds(i * size, size)
        out_ref[rows, :] = (1.0 - alpha_mix) * total + alpha_mix * first_ref[rows, :].astype(f32)


def stale_mixture(first_rows, stale, tiles, sources):
    return pl.pallas_call(
        stale_kernel,
        in_specs=[vmem] * 3 + [smem],
        out_specs=vmem,
        out_shape=pltpu.HBM(first_rows.shape, f32),
        compiler_params=params(),
        cost_estimate=cost(140 * 1000 * 1000, 4 * 1024 * 1024),
        name="stale_mixture",
    )(first_rows, stale, tiles, sources)


def second_kernel(sources_ref, group_ref, hidden_ref, stale_ref, tiles_ref, *refs):
    index_refs, (rounded_ref, columns_ref, low_ref, high_ref) = refs[:-4], refs[-4:]
    groups = len(index_refs)
    targets = index_refs[0].shape[0] // 2
    size = tiles_ref.shape[2]
    for i in range(tiles_ref.shape[0]):
        rows = pl.ds(i * size, size)
        total = local_sum(tiles_ref, sources_ref, hidden_ref.at[0], i)
        rounded_ref[rows, :] = ((1.0 - alpha_mix) * total + stale_ref[rows, :]).astype(bf16)
    for k, ref in enumerate(index_refs):
        source = lax.rem(group_ref[0] + groups - k, groups)
        span = pl.ds(pl.multiple_of(source * targets, targets), targets)
        place = ref[...].astype(f32)
        low_ref[span, :] = place[:targets]
        high_ref[span, :] = place[targets:]
    columns_ref[0] = turned(low_ref[...]).astype(bf16)
    columns_ref[1] = turned(high_ref[...]).astype(bf16)


def second_mixture(group, hidden_copies, stale_mixed, tiles, sources, index):
    shape = stale_mixed.shape
    used = len(index) * index[0].shape[0] // 2
    square = (2, shape[1], shape[1])
    return pl.pallas_call(
        second_kernel,
        grid=(1,),
        in_specs=[smem] * 2
        + [
            pl.BlockSpec((1,) + shape, lambda g: (0, 0, 0)),
            pl.BlockSpec(shape, lambda g: (0, 0)),
            pl.BlockSpec((tiles.shape[0], 2) + tiles.shape[2:], lambda g: (0, 0, 0, 0)),
        ]
        + [pl.BlockSpec(index[0].shape, lambda g: (0, 0))] * len(index),
        out_specs=[pl.BlockSpec(shape, lambda g: (0, 0)), pl.BlockSpec(square, lambda g: (0, 0, 0))],
        out_shape=[jax.ShapeDtypeStruct(shape, bf16), jax.ShapeDtypeStruct(square, bf16)],
        scratch_shapes=[pltpu.VMEM((used, shape[1]), f32)] * 2,
        compiler_params=params(),
        cost_estimate=cost(34 * 1000 * 1000, 2 * 1024 * 1024),
        name="second_mixture",
    )(sources, group, *in_hbm(hidden_copies, stale_mixed, tiles), *index)


def columns_of(weight_ref, layer):
    half = weight_ref.shape[1] // 2
    return lambda z: weight_ref[z, pl.ds(layer * half, half), :]


def finished(beta, parts, own, weight_of):
    turned = None
    for (z, first), (zz, second) in zip(parts[::2], parts[1::2]):
        left = jnp.concatenate([first, second], axis=1)
        right = jnp.concatenate([weight_of(z), weight_of(zz)], axis=1)
        term = dot_nt(left, right)
        turned = term if turned is None else turned + term
    return jax.nn.relu((1.0 - beta) * own.astype(f32) + beta * turned).astype(bf16)


def hidden_kernel(place_ref, parts_ref, weight_ref, out_ref, hidden_ref, sems):
    parts = [(z, parts_ref[z]) for z in range(parts_ref.shape[0])]
    hidden_ref[...] = finished(beta_first, parts, parts_ref[place_ref[0]], columns_of(weight_ref, 0))
    copies = [
        pltpu.make_async_copy(hidden_ref, out_ref.at[g], sems.at[g]) for g in range(out_ref.shape[0])
    ]
    for copy in copies:
        copy.start()
    for copy in copies:
        copy.wait()


def hidden_copies(place, parts, weights, groups):
    shape = parts.shape[1:]
    return pl.pallas_call(
        hidden_kernel,
        in_specs=[smem] + [vmem] * 2,
        out_specs=pl.BlockSpec(memory_space=pltpu.HBM),
        out_shape=pltpu.HBM((groups,) + shape, bf16),
        scratch_shapes=[pltpu.VMEM(shape, bf16), pltpu.SemaphoreType.DMA((groups,))],
        compiler_params=params(),
        cost_estimate=cost(134 * 1000 * 1000, 3 * 1024 * 1024),
        name="hidden",
    )(place, parts, weights)


def final_kernel(places, place_ref, weight_ref, *refs):
    feats = len(places)
    parts = [(lax.rem(place_ref[0] + (feats - k), feats), ref[...]) for k, ref in zip(places, refs)]
    refs[-1][...] = finished(beta_second, parts, refs[0][...], columns_of(weight_ref, 1))


def final_rows(place, weights, parts):
    places = list(parts)

    def kernel(*refs):
        final_kernel(places, *refs)

    return pl.pallas_call(
        kernel,
        in_specs=[smem] + [vmem] * (1 + len(parts)),
        out_specs=vmem,
        out_shape=jax.ShapeDtypeStruct(parts[0].shape, bf16),
        compiler_params=params(),
        cost_estimate=cost(134 * 1000 * 1000, 3 * 1024 * 1024),
        name="final_rows",
    )(place, weights, *parts.values())


def compact_kernel(groups, peers_ref, arrived_ref, out_ref, sems):
    ranks = arrived_ref.shape[0] // groups
    copies = [
        pltpu.make_async_copy(
            arrived_ref.at[arrival(peers_ref[j], ranks, groups)], out_ref.at[j], sems.at[j]
        )
        for j in range(out_ref.shape[0])
    ]
    for copy in copies:
        copy.start()
    for copy in copies:
        copy.wait()


def compact(arrived, peers, groups):
    shape = (peers.shape[0],) + arrived.shape[1:]

    def kernel(*refs):
        compact_kernel(groups, *refs)

    out = pl.pallas_call(
        kernel,
        in_specs=[smem, vmem],
        out_specs=pl.BlockSpec(memory_space=pl.ANY),
        out_shape=jax.ShapeDtypeStruct(shape, arrived.dtype),
        scratch_shapes=[pltpu.SemaphoreType.DMA((shape[0],))],
        compiler_params=params(),
        cost_estimate=cost(0, 2 * 1024 * 1024),
        name="compact",
    )(peers, arrived)
    return out.reshape(-1, arrived.shape[2])


def slab_columns(w_first, w_second, feats):
    both = jnp.concatenate([w_first.T, w_second.T], axis=0)
    pairs = [
        ((z * RANKS + r) * feats + y, (y * RANKS + r) * feats + z)
        for z in range(feats)
        for r in range(RANKS)
        for y in range(feats)
    ]
    both = lax.ppermute(both, ("dom", "feat"), pairs)
    slabs = [[z * RANKS + r for r in range(RANKS)] for z in range(feats)]
    got = lax.all_gather(both, "dom", axis=0, tiled=True, axis_index_groups=slabs)
    return got.reshape(RANKS, 2, -1, both.shape[1]).swapaxes(0, 1).reshape(got.shape)


def own_columns(rows, feats):
    pairs = [[(z + e) * RANKS + r for e in (0, 1)] for z in range(0, feats, 2) for r in range(RANKS)]
    strides = [[z * RANKS + r for z in range(e, feats, 2)] for e in (0, 1) for r in range(RANKS)]
    both = lax.all_gather(rows, "dom", axis=0, tiled=True, axis_index_groups=pairs)
    got = lax.all_gather(both, "dom", axis=0, tiled=True, axis_index_groups=strides)
    return got.reshape(feats, -1, rows.shape[1])


def swap(blocks, axis, groups=None):
    return lax.all_to_all(blocks, axis, split_axis=0, concat_axis=0, axis_index_groups=groups, tiled=True)


def moved(rows, axis, by):
    size = lax.axis_size(axis)
    return lax.ppermute(rows, axis, [(i, (i + by) % size) for i in range(size)])


def shards(
    first_layer,
    w_first,
    w_second,
    tile_values,
    tile_sources,
    halo_sources,
    send_rows,
    block_counts,
    stale_halo,
):
    count = first_layer.shape[0]
    picks = send_rows[0]
    feats = lax.axis_size("feat")
    sources = tile_sources[0]
    listed = halo_sources[0]
    stale = stale_halo.reshape(listed.shape[0], picks.shape[1], -1)
    near = 2 * RANKS
    groups = picks.shape[0] // near
    far_groups = [[a * near + m for a in range(groups)] for m in range(near)]
    near_groups = [[a * near + m for m in range(near)] for a in range(groups)]
    place = lax.axis_index("feat").astype(i32).reshape(1)
    group = (lax.axis_index("dom") // near).astype(i32).reshape(1)

    leaving, index = pack_first(first_layer, picks, block_counts, groups)
    leaving, index, w_first, w_second, stale = lax.optimization_barrier(
        (leaving, index, w_first, w_second, stale)
    )
    index = [
        lax.dynamic_index_in_dim(index, lax.rem(group[0] + k, groups), keepdims=False) for k in range(groups)
    ]
    index = index[:1] + [moved(index[k], "dom", k * near) for k in range(1, groups)]
    slab = slab_columns(w_first, w_second, feats)
    arrived = swap(leaving, "dom")
    stale_mixed = stale_mixture(first_layer, stale, tile_values, sources)
    rounded = first_mixture(first_layer, arrived, tile_values, sources, listed, feats)
    rounded, slab, stale_mixed, *index = lax.optimization_barrier((rounded, slab, stale_mixed, *index))
    parts = swap(rounded, "feat")
    weights = own_columns(slab, feats)

    hidden = hidden_copies(place, parts, weights, groups)
    spread_hidden = swap(hidden, "dom", far_groups)
    own, columns = second_mixture(group, hidden, stale_mixed, tile_values, sources, index)
    before, after = moved(own, "feat", 1), moved(own, "feat", -1)
    blocks = pack_second(spread_hidden, columns, near)
    blocks, before, after = lax.optimization_barrier((blocks, before, after))
    received = swap(blocks, "dom", near_groups).reshape((-1,) + blocks.shape[2:])
    parts = {0: own, 1: before, -1: after}
    parts.update({4: moved(before, "feat", 3), 3: moved(before, "feat", 2), -3: moved(after, "feat", -2)})
    parts.update({2: moved(before, "feat", 1), -2: moved(after, "feat", -1)})
    layer_out = final_rows(place, weights, parts)
    fresh_halo = compact(received, listed, groups)
    return (layer_out, fresh_halo)


def solution(mesh):
    placed = (
        P("dom", "feat"),
        P("feat", "dom"),
        P("feat", "dom"),
        P("dom", None, None, None),
        P("dom", None, None),
        P("dom", None),
        P("dom", None, None),
        P("dom", None),
        P("dom", "feat"),
    )
    return jax.shard_map(
        shards,
        mesh=mesh,
        in_specs=placed,
        out_specs=(P("dom", "feat"), P("dom", "feat")),
        check_vma=False,
    )
```

```python
import math

import jax
import jax.numpy as jnp
from jax import lax
from jax.experimental import pallas as pl
from jax.experimental.pallas import tpu as pltpu
from jax.sharding import PartitionSpec as P

alpha_mix = 0.1
beta_first = math.log(1.5)
beta_second = math.log(1.25)
VMEM_BYTES = 16 * 1024 * 1024
RANKS = 8
SEND = 8
GROUP = 2
bf16 = jnp.bfloat16
f32 = jnp.float32
i32 = jnp.int32
vmem = pl.BlockSpec(memory_space=pltpu.VMEM)
smem = pl.BlockSpec(memory_space=pltpu.SMEM)


def params(limit=VMEM_BYTES):
    return pltpu.CompilerParams(vmem_limit_bytes=limit)


def cost(flops, moved):
    return pl.CostEstimate(flops=flops, bytes_accessed=moved, transcendentals=0)


def in_hbm(*arrays):
    return [pltpu.with_memory_space_constraint(array, pltpu.HBM) for array in arrays]


def dot_nt(left, right):
    return lax.dot_general(left, right, (((1,), (1,)), ((), ())), preferred_element_type=f32)


def fold_rows(rows):
    half = rows.shape[0] // 2
    return jnp.concatenate([rows[:half], rows[half:]], axis=1)


def place_of(picks, counts, half):
    targets = picks.shape[0]
    square = (targets, targets)
    same = lax.broadcasted_iota(i32, square, 0) == lax.broadcasted_iota(i32, square, 1)
    listed = jnp.where(same, jnp.broadcast_to(counts, square), 0)
    listed = jnp.sum(listed, axis=1, keepdims=True)
    high = picks >= half
    live = jnp.logical_and(listed > 0, picks < 2 * half)
    low = jnp.where(live, picks - jnp.where(high, half, 0), half + 44)
    return low.astype(f32), jnp.where(high, 1.0, 0.0)


def turned(rows):
    return jnp.concatenate([rows] * (rows.shape[1] // rows.shape[0]), axis=0).T


def picker(half, slots, width):
    lanes = slots
    places = [
        (lax.broadcasted_iota(i32, (slots, lanes), 1) + first).astype(f32).astype(bf16)
        for first in range(0, half, lanes)
    ]
    one, zero = jnp.ones((slots, lanes), bf16), jnp.zeros((slots, lanes), bf16)

    def pick(folded, low, high):
        wanted = jnp.broadcast_to(low, (slots, lanes)).astype(bf16)
        hot = jnp.concatenate([jnp.where(wanted == place, one, zero) for place in places], axis=1)
        both = jnp.dot(hot, folded, preferred_element_type=f32)
        side = jnp.broadcast_to(high, (slots, width))
        return jnp.where(side > 0.5, both[:, width:], both[:, :width]).astype(bf16)

    return pick


def pack_first_kernel(rows_ref, picks_ref, counts_ref, out_ref, index_ref, blocks_ref, places_ref, sems):
    targets, slots, width = blocks_ref.shape
    groups = index_ref.shape[0]
    half = rows_ref.shape[0] // 2
    low, high = place_of(picks_ref[...], counts_ref[...], half)
    per = targets // groups
    for g in range(groups):
        places_ref[g, 0:per, :] = low[g * per : (g + 1) * per].astype(bf16)
        places_ref[g, per : 2 * per, :] = high[g * per : (g + 1) * per].astype(bf16)
    copies = [pltpu.make_async_copy(places_ref, index_ref, sems.at[targets // SEND])]
    copies[0].start()
    low, high = turned(low), turned(high)
    folded = fold_rows(rows_ref[...])
    pick = picker(half, slots, width)
    for t in range(targets):
        blocks_ref[t] = pick(folded, low[:, t : t + 1], high[:, t : t + 1])
        if (t + 1) % SEND == 0:
            span = pl.ds(t + 1 - SEND, SEND)
            copies.append(pltpu.make_async_copy(blocks_ref.at[span], out_ref.at[span], sems.at[t // SEND]))
            copies[-1].start()
    for copy in copies:
        copy.wait()


def pack_first(rows, picks, counts, groups):
    targets, slots = picks.shape
    count, width = rows.shape
    index = (groups, 2 * targets // groups, slots)
    return pl.pallas_call(
        pack_first_kernel,
        in_specs=[vmem] * 3,
        out_specs=[pl.BlockSpec(memory_space=pltpu.HBM)] * 2,
        out_shape=[pltpu.HBM((targets, slots, width), bf16), pltpu.HBM(index, bf16)],
        scratch_shapes=[
            pltpu.VMEM((targets, slots, width), bf16),
            pltpu.VMEM(index, bf16),
            pltpu.SemaphoreType.DMA((targets // SEND + 1,)),
        ],
        compiler_params=params(),
        cost_estimate=cost(2 * targets * slots * count * width, 3 * 1024 * 1024),
        name="pack_first",
    )(*in_hbm(rows, picks, counts))


def pack_second_kernel(rows_ref, columns_ref, out_ref, blocks_ref, sems):
    targets, groups, slots, width = blocks_ref.shape
    low, high = columns_ref[0].astype(f32), columns_ref[1].astype(f32)
    folded = [fold_rows(rows_ref[a]) for a in range(groups)]
    pick = picker(rows_ref.shape[1] // 2, slots, width)
    copies = []
    for t in range(targets):
        for a in range(groups):
            c = a * targets + t
            blocks_ref[t, a] = pick(folded[a], low[:, c : c + 1], high[:, c : c + 1])
        if (t + 1) % GROUP == 0:
            span = pl.ds(t + 1 - GROUP, GROUP)
            copies.append(pltpu.make_async_copy(blocks_ref.at[span], out_ref.at[span], sems.at[t // GROUP]))
            copies[-1].start()
    for copy in copies:
        copy.wait()


def pack_second(rows, columns, targets):
    groups, count, width = rows.shape
    shape = (targets, groups, width, width)
    return pl.pallas_call(
        pack_second_kernel,
        in_specs=[vmem] * 2,
        out_specs=pl.BlockSpec(memory_space=pltpu.HBM),
        out_shape=pltpu.HBM(shape, bf16),
        scratch_shapes=[pltpu.VMEM(shape, bf16), pltpu.SemaphoreType.DMA((shape[0] // GROUP,))],
        compiler_params=params(),
        cost_estimate=cost(2 * shape[0] * groups * width * count * width, 3 * 1024 * 1024),
        name="pack_second",
    )(rows, columns)


def arrival(source, ranks, groups):
    return lax.rem(source, ranks) * groups + lax.div(source, ranks)


def tile_pairs(tiles_ref, i, firsts, block):
    total = None
    for k in firsts:
        left = jnp.concatenate([tiles_ref[i, k], tiles_ref[i, k + 1]], axis=1)
        right = jnp.concatenate([block(i, k), block(i, k + 1)], axis=0)
        term = jnp.dot(left, right, preferred_element_type=f32)
        total = term if total is None else total + term
    return total


def local_sum(tiles_ref, sources_ref, local_ref, i):
    size = tiles_ref.shape[2]

    def block(i, k):
        return local_ref[pl.ds(pl.multiple_of(sources_ref[i, k] * size, size), size), :]

    return tile_pairs(tiles_ref, i, [0], block)


def halo_sum(tiles_ref, sources_ref, block_of, i):
    blocks, tiles = tiles_ref.shape[0], tiles_ref.shape[1]

    def block(i, k):
        return block_of(sources_ref[i, k] - blocks)

    return tile_pairs(tiles_ref, i, range(2, tiles, 2), block)


def first_kernel(local_ref, halo_ref, tiles_ref, sources_ref, peers_ref, out_ref, rounded_ref, sems):
    size = tiles_ref.shape[2]
    blocks = tiles_ref.shape[0]
    copies = []
    for i in range(blocks):
        total = local_sum(tiles_ref, sources_ref, local_ref, i)
        total = total + halo_sum(tiles_ref, sources_ref, lambda j: halo_ref[peers_ref[j]], i)
        rows = pl.ds(i * size, size)
        mixed = (1.0 - alpha_mix) * total + alpha_mix * local_ref[rows, :].astype(f32)
        rounded_ref[rows, :] = mixed.astype(bf16)
        if i % 2 == 1:
            ready = pl.ds((i - 1) * size, 2 * size)
            for g in range(out_ref.shape[0]):
                copy = pltpu.make_async_copy(rounded_ref.at[ready], out_ref.at[g, ready], sems.at[i // 2, g])
                copy.start()
                copies.append(copy)
    for copy in copies:
        copy.wait()


def first_mixture(rows, halo, tiles, sources, peers, copies):
    count, width = rows.shape
    return pl.pallas_call(
        first_kernel,
        in_specs=[vmem] * 3 + [smem] * 2,
        out_specs=pl.BlockSpec(memory_space=pltpu.HBM),
        out_shape=pltpu.HBM((copies, count, width), bf16),
        scratch_shapes=[pltpu.VMEM((count, width), bf16), pltpu.SemaphoreType.DMA((tiles.shape[0] // 2, copies))],
        compiler_params=params(),
        cost_estimate=cost(170 * 1000 * 1000, 5 * 1024 * 1024),
        name="first_mixture",
    )(rows, halo, tiles, sources, peers)


def stale_kernel(first_ref, stale_ref, tiles_ref, sources_ref, out_ref):
    size = tiles_ref.shape[2]
    for i in range(tiles_ref.shape[0]):
        total = halo_sum(tiles_ref, sources_ref, lambda j: stale_ref[j], i)
        rows = pl.ds(i * size, size)
        out_ref[rows, :] = (1.0 - alpha_mix) * total + alpha_mix * first_ref[rows, :].astype(f32)


def stale_mixture(first_rows, stale, tiles, sources):
    return pl.pallas_call(
        stale_kernel,
        in_specs=[vmem] * 3 + [smem],
        out_specs=vmem,
        out_shape=pltpu.HBM(first_rows.shape, f32),
        compiler_params=params(),
        cost_estimate=cost(140 * 1000 * 1000, 4 * 1024 * 1024),
        name="stale_mixture",
    )(first_rows, stale, tiles, sources)


def second_kernel(sources_ref, group_ref, hidden_ref, stale_ref, tiles_ref, *refs):
    index_refs, (rounded_ref, columns_ref, low_ref, high_ref) = refs[:-4], refs[-4:]
    groups = len(index_refs)
    targets = index_refs[0].shape[0] // 2
    size = tiles_ref.shape[2]
    for i in range(tiles_ref.shape[0]):
        rows = pl.ds(i * size, size)
        total = local_sum(tiles_ref, sources_ref, hidden_ref.at[0], i)
        rounded_ref[rows, :] = ((1.0 - alpha_mix) * total + stale_ref[rows, :]).astype(bf16)
    for k, ref in enumerate(index_refs):
        source = lax.rem(group_ref[0] + groups - k, groups)
        span = pl.ds(pl.multiple_of(source * targets, targets), targets)
        place = ref[...].astype(f32)
        low_ref[span, :] = place[:targets]
        high_ref[span, :] = place[targets:]
    columns_ref[0] = turned(low_ref[...]).astype(bf16)
    columns_ref[1] = turned(high_ref[...]).astype(bf16)


def second_mixture(group, hidden_copies, stale_mixed, tiles, sources, index):
    shape = stale_mixed.shape
    used = len(index) * index[0].shape[0] // 2
    square = (2, shape[1], shape[1])
    return pl.pallas_call(
        second_kernel,
        grid=(1,),
        in_specs=[smem] * 2
        + [
            pl.BlockSpec((1,) + shape, lambda g: (0, 0, 0)),
            pl.BlockSpec(shape, lambda g: (0, 0)),
            pl.BlockSpec((tiles.shape[0], 2) + tiles.shape[2:], lambda g: (0, 0, 0, 0)),
        ]
        + [pl.BlockSpec(index[0].shape, lambda g: (0, 0))] * len(index),
        out_specs=[pl.BlockSpec(shape, lambda g: (0, 0)), pl.BlockSpec(square, lambda g: (0, 0, 0))],
        out_shape=[jax.ShapeDtypeStruct(shape, bf16), jax.ShapeDtypeStruct(square, bf16)],
        scratch_shapes=[pltpu.VMEM((used, shape[1]), f32)] * 2,
        compiler_params=params(),
        cost_estimate=cost(34 * 1000 * 1000, 2 * 1024 * 1024),
        name="second_mixture",
    )(sources, group, *in_hbm(hidden_copies, stale_mixed, tiles), *index)


def columns_of(weight_ref, layer):
    half = weight_ref.shape[1] // 2
    return lambda z: weight_ref[z, pl.ds(layer * half, half), :]


def finished(beta, parts, own, weight_of):
    turned = None
    for (z, first), (zz, second) in zip(parts[::2], parts[1::2]):
        left = jnp.concatenate([first, second], axis=1)
        right = jnp.concatenate([weight_of(z), weight_of(zz)], axis=1)
        term = dot_nt(left, right)
        turned = term if turned is None else turned + term
    return jax.nn.relu((1.0 - beta) * own.astype(f32) + beta * turned).astype(bf16)


def hidden_kernel(place_ref, parts_ref, weight_ref, out_ref, hidden_ref, sems):
    parts = [(z, parts_ref[z]) for z in range(parts_ref.shape[0])]
    hidden_ref[...] = finished(beta_first, parts, parts_ref[place_ref[0]], columns_of(weight_ref, 0))
    copies = [
        pltpu.make_async_copy(hidden_ref, out_ref.at[g], sems.at[g]) for g in range(out_ref.shape[0])
    ]
    for copy in copies:
        copy.start()
    for copy in copies:
        copy.wait()


def hidden_copies(place, parts, weights, groups):
    shape = parts.shape[1:]
    return pl.pallas_call(
        hidden_kernel,
        in_specs=[smem] + [vmem] * 2,
        out_specs=pl.BlockSpec(memory_space=pltpu.HBM),
        out_shape=pltpu.HBM((groups,) + shape, bf16),
        scratch_shapes=[pltpu.VMEM(shape, bf16), pltpu.SemaphoreType.DMA((groups,))],
        compiler_params=params(),
        cost_estimate=cost(134 * 1000 * 1000, 3 * 1024 * 1024),
        name="hidden",
    )(place, parts, weights)


def final_kernel(places, place_ref, weight_ref, *refs):
    feats = len(places)
    parts = [(lax.rem(place_ref[0] + (feats - k), feats), ref[...]) for k, ref in zip(places, refs)]
    refs[-1][...] = finished(beta_second, parts, refs[0][...], columns_of(weight_ref, 1))


def final_rows(place, weights, parts):
    places = list(parts)

    def kernel(*refs):
        final_kernel(places, *refs)

    return pl.pallas_call(
        kernel,
        in_specs=[smem] + [vmem] * (1 + len(parts)),
        out_specs=vmem,
        out_shape=jax.ShapeDtypeStruct(parts[0].shape, bf16),
        compiler_params=params(),
        cost_estimate=cost(134 * 1000 * 1000, 3 * 1024 * 1024),
        name="final_rows",
    )(place, weights, *parts.values())


def compact_kernel(groups, peers_ref, arrived_ref, out_ref, sems):
    ranks = arrived_ref.shape[0] // groups
    copies = [
        pltpu.make_async_copy(
            arrived_ref.at[arrival(peers_ref[j], ranks, groups)], out_ref.at[j], sems.at[j]
        )
        for j in range(out_ref.shape[0])
    ]
    for copy in copies:
        copy.start()
    for copy in copies:
        copy.wait()


def compact(arrived, peers, groups):
    shape = (peers.shape[0],) + arrived.shape[1:]

    def kernel(*refs):
        compact_kernel(groups, *refs)

    out = pl.pallas_call(
        kernel,
        in_specs=[smem, vmem],
        out_specs=pl.BlockSpec(memory_space=pl.ANY),
        out_shape=jax.ShapeDtypeStruct(shape, arrived.dtype),
        scratch_shapes=[pltpu.SemaphoreType.DMA((shape[0],))],
        compiler_params=params(),
        cost_estimate=cost(0, 2 * 1024 * 1024),
        name="compact",
    )(peers, arrived)
    return out.reshape(-1, arrived.shape[2])


def slab_columns(w_first, w_second, feats):
    both = jnp.concatenate([w_first.T, w_second.T], axis=0)
    pairs = [
        ((z * RANKS + r) * feats + y, (y * RANKS + r) * feats + z)
        for z in range(feats)
        for r in range(RANKS)
        for y in range(feats)
    ]
    both = lax.ppermute(both, ("dom", "feat"), pairs)
    slabs = [[z * RANKS + r for r in range(RANKS)] for z in range(feats)]
    got = lax.all_gather(both, "dom", axis=0, tiled=True, axis_index_groups=slabs)
    return got.reshape(RANKS, 2, -1, both.shape[1]).swapaxes(0, 1).reshape(got.shape)


def own_columns(rows, feats):
    pairs = [[(z + e) * RANKS + r for e in (0, 1)] for z in range(0, feats, 2) for r in range(RANKS)]
    strides = [[z * RANKS + r for z in range(e, feats, 2)] for e in (0, 1) for r in range(RANKS)]
    both = lax.all_gather(rows, "dom", axis=0, tiled=True, axis_index_groups=pairs)
    got = lax.all_gather(both, "dom", axis=0, tiled=True, axis_index_groups=strides)
    return got.reshape(feats, -1, rows.shape[1])


def swap(blocks, axis, groups=None):
    return lax.all_to_all(blocks, axis, split_axis=0, concat_axis=0, axis_index_groups=groups, tiled=True)


def moved(rows, axis, by):
    size = lax.axis_size(axis)
    return lax.ppermute(rows, axis, [(i, (i + by) % size) for i in range(size)])


def shards(
    first_layer,
    w_first,
    w_second,
    tile_values,
    tile_sources,
    halo_sources,
    send_rows,
    block_counts,
    stale_halo,
):
    count = first_layer.shape[0]
    picks = send_rows[0]
    feats = lax.axis_size("feat")
    sources = tile_sources[0]
    listed = halo_sources[0]
    stale = stale_halo.reshape(listed.shape[0], picks.shape[1], -1)
    near = 2 * RANKS
    groups = picks.shape[0] // near
    far_groups = [[a * near + m for a in range(groups)] for m in range(near)]
    near_groups = [[a * near + m for m in range(near)] for a in range(groups)]
    place = lax.axis_index("feat").astype(i32).reshape(1)
    group = (lax.axis_index("dom") // near).astype(i32).reshape(1)

    leaving, index = pack_first(first_layer, picks, block_counts, groups)
    leaving, index, w_first, w_second, stale = lax.optimization_barrier(
        (leaving, index, w_first, w_second, stale)
    )
    index = [
        lax.dynamic_index_in_dim(index, lax.rem(group[0] + k, groups), keepdims=False) for k in range(groups)
    ]
    index = index[:1] + [moved(index[k], "dom", k * near) for k in range(1, groups)]
    slab = slab_columns(w_first, w_second, feats)
    arrived = swap(leaving, "dom")
    stale_mixed = stale_mixture(first_layer, stale, tile_values, sources)
    rounded = first_mixture(first_layer, arrived, tile_values, sources, listed, feats)
    rounded, slab, stale_mixed, *index = lax.optimization_barrier((rounded, slab, stale_mixed, *index))
    parts = swap(rounded, "feat")
    weights = own_columns(slab, feats)

    hidden = hidden_copies(place, parts, weights, groups)
    spread_hidden = swap(hidden, "dom", far_groups)
    own, columns = second_mixture(group, hidden, stale_mixed, tile_values, sources, index)
    before = moved(own, "feat", 1)
    blocks = pack_second(spread_hidden, columns, near)
    blocks, before, own = lax.optimization_barrier((blocks, before, own))
    received = swap(blocks, "dom", near_groups).reshape((-1,) + blocks.shape[2:])
    parts = {0: own, 1: before}
    parts.update({4: moved(before, "feat", 3), -3: moved(own, "feat", -3), 3: moved(before, "feat", 2)})
    parts.update({-2: moved(own, "feat", -2), 2: moved(before, "feat", 1), -1: moved(own, "feat", -1)})
    layer_out = final_rows(place, weights, parts)
    fresh_halo = compact(received, listed, groups)
    return (layer_out, fresh_halo)


def solution(mesh):
    placed = (
        P("dom", "feat"),
        P("feat", "dom"),
        P("feat", "dom"),
        P("dom", None, None, None),
        P("dom", None, None),
        P("dom", None),
        P("dom", None, None),
        P("dom", None),
        P("dom", "feat"),
    )
    return jax.shard_map(
        shards,
        mesh=mesh,
        in_specs=placed,
        out_specs=(P("dom", "feat"), P("dom", "feat")),
        check_vma=False,
    )
```
